128 devices in a mesh: row: 8 (over z_lo, y), col: 16 (over x, z_hi, core).
Axes of the slice: x: 4, y: 4, z: 4 (z_hi: 2, z_lo: 2; z = z_hi * 2 + z_lo), core: 2. Of those that a mesh axis runs over, the one named last changes fastest.
Arguments:
- pressure: float32 [512, 256, 512], P('row', 'col'), may hold values from -4.5 to 4.5
- pressure_prior: float32 [512, 256, 512], P('row', 'col'), may hold values from -6 to 6
- lossy_prior: float32 [512, 256, 512], P('row', 'col'), may hold values from -12 to 12
- stiffness: float32 [512, 256, 512], P('row', 'col'), may hold values from 0.01 to 0.05
- compensation: float32 [512, 256, 512], P('row', 'col'), may hold values from 0.05 to 0.2
- snapshot: float32 [512, 256, 512], P('row', 'col'), may hold values from -6 to 6
- image_prior: float32 [512, 256, 512], P('row', 'col'), may hold values from -6 to 6
Outputs:
- pressure_next: float32 [512, 256, 512], P('row', 'col')
- lossy_term: float32 [512, 256, 512], P('row', 'col')
- image_sum: float32 [512, 256, 512], P('row', 'col')
The draws below stay inside these ranges and needn't reach their ends.
All inputs are finite; a program needn't handle non-finite values.
Results may differ from the reference program's by a relative error of at most 0.00013.
Values sent between devices are 32-bit elements; how exact they have to be, the bound alone decides.
No kernel may reach another device: no remote copies, remote signals or barrier semaphores. Data moves between devices by JAX's collectives and lax.ppermute only.
A program may use at most 128 MiB of HBM per device.

```python
import math
import jax
import jax.numpy as jnp

NX = 512
NY = 512
NZ = 256


def draw_pressure(key, part):
    key = jax.random.fold_in(key, 11)
    values = jax.random.normal(key, (NY, NZ, NX), jnp.float32)
    return jnp.clip(values, -4.5, 4.5)


def steps_of(stream_key, dims, cuts, low, high):
    def one(dim, blocks):
        steps = jax.random.uniform(jax.random.fold_in(jax.random.fold_in(stream_key, 6), dim), (blocks,), jnp.float32, low / len(cuts), high / len(cuts))
        return jnp.repeat(jnp.exp(steps), dims[dim] // blocks).reshape((-1,) + (1,) * (len(dims) - dim - 1))

    level = one(*cuts[0])
    for cut in cuts[1:]:
        level = level * one(*cut)
    return level


def noise(rng, shape, deviation, bound, cuts=(), kind=jnp.bfloat16):
    drawn = jax.random.normal(rng, shape, jnp.float32) * deviation
    if len(cuts) > 0:
        drawn = steps_of(rng, shape, cuts, -0.22, 0.18) * drawn
    return jnp.clip(drawn, min=-bound, max=bound).astype(kind)


def setup_inputs(seed: int = 0) -> dict:
    streams_of = jax.random.split(jax.random.key(seed), 8)
    return {
        "pressure": draw_pressure(jax.random.fold_in(streams_of[7], 71), 0),
        "pressure_prior": noise(streams_of[1], (NY, NZ, NX), 1.0, 6.0, ((0, 8), (1, 16)), jnp.float32),
        "lossy_prior": noise(streams_of[2], (NY, NZ, NX), 2.0, 12.0, ((0, 8), (1, 16)), jnp.float32),
        "stiffness": jnp.clip(jnp.exp(math.log(0.05) - 1.609438 * jax.random.uniform(streams_of[3], (NY, NZ, NX), jnp.float32) ** steps_of(streams_of[3], (NY, NZ, NX), ((0, 8), (1, 16)), -0.2, 0.2)), 0.01, 0.05),
        "compensation": jnp.clip(jnp.exp(math.log(0.2) - 1.3862944 * jax.random.uniform(streams_of[4], (NY, NZ, NX), jnp.float32) ** steps_of(streams_of[4], (NY, NZ, NX), ((0, 8), (1, 16)), -0.2, 0.2)), 0.05, 0.2),
        "snapshot": noise(streams_of[5], (NY, NZ, NX), 1.0, 6.0, ((0, 8), (1, 16)), jnp.float32),
        "image_prior": noise(streams_of[6], (NY, NZ, NX), 1.0, 6.0, ((0, 8), (1, 16)), jnp.float32),
    }


stiff_power = 1.03
lossy_power = 0.53
filter_rate = 0.14


def wavenumber(count):
    indices = jnp.arange(count, dtype=jnp.int32)
    folded = jnp.minimum(indices, count - indices)
    return (2.0 * math.pi / count) * folded.astype(jnp.float32)


def reference(pressure, pressure_prior, lossy_prior, stiffness, compensation, snapshot, image_prior):
    wave_y = wavenumber(NY)
    wave_z = wavenumber(NZ)
    wave_x = (2.0 * math.pi / NX) * jnp.arange(NX // 2 + 1, dtype=jnp.int32).astype(jnp.float32)
    squared = wave_y[:, None, None] ** 2 + wave_z[None, :, None] ** 2 + wave_x[None, None, :] ** 2
    stiff_mult = squared ** stiff_power
    lossy_mult = squared ** lossy_power * jnp.exp(-filter_rate * squared)
    spectrum = jnp.fft.rfftn(pressure)
    stiff_term = jnp.fft.irfftn(spectrum * stiff_mult, s=pressure.shape).astype(jnp.float32)
    lossy_term = jnp.fft.irfftn(spectrum * lossy_mult, s=pressure.shape).astype(jnp.float32)
    pressure_next = 2.0 * pressure - pressure_prior - stiffness * stiff_term + compensation * (lossy_term - lossy_prior)
    image_sum = image_prior + snapshot * pressure_next
    return pressure_next, lossy_term, image_sum
```

```python
import functools
import math

import jax
import jax.numpy as jnp
import ml_dtypes
import numpy as np
from jax import lax
from jax.experimental import pallas as pl
from jax.experimental.pallas import tpu as pltpu
from jax.sharding import PartitionSpec as P

stiff_power = 1.03
lossy_power = 0.53
filter_rate = 0.14
MIB = 1 << 20


def split_table(table):
    high = table.astype(ml_dtypes.bfloat16)
    low = (table - high.astype(np.float64)).astype(ml_dtypes.bfloat16)
    return high, low


def cas(left, right, length):
    angle = 2.0 * math.pi / length * (np.outer(left, right) % length)
    return np.cos(angle) + np.sin(angle)


def left_table(table):
    high, low = split_table(table)
    return np.concatenate([high, high, low], axis=1)


def right_table(table):
    high, low = split_table(table)
    return np.concatenate([high, high, low], axis=0)


def pieces(values):
    high = values.astype(jnp.bfloat16)
    low = (values - high.astype(jnp.float32)).astype(jnp.bfloat16)
    return high, low


def times_table(values, table):
    high, low = pieces(values)
    return jnp.dot(jnp.concatenate([high, low, high], axis=1), table, preferred_element_type=jnp.float32)


def table_times(table, values):
    high, low = pieces(values)
    return jnp.dot(table, jnp.concatenate([high, low, high], axis=0), preferred_element_type=jnp.float32)


def table_times_rows(table, values):
    high, low = pieces(values)
    return lax.dot_general(
        table,
        jnp.concatenate([high, low, high], axis=1),
        (((1,), (1,)), ((), ())),
        preferred_element_type=jnp.float32,
    )


def swap_halves(first, second):
    lane = lax.broadcasted_iota(jnp.int32, first.shape, 1)
    left = jnp.where(lane < 64, first, pltpu.roll(second, 64, 1))
    right = jnp.where(lane < 64, pltpu.roll(first, 64, 1), second)
    return left, right


def side(parts):
    return jnp.concatenate(parts, axis=1)


def forward_x_kernel(pressure, even_left, odd_left, sent, field, packed, in_sems, out_sems):
    def load(h, g):
        return pltpu.make_async_copy(
            pressure.at[:, h, :, pl.ds(g * 128, 128)], field.at[h, g], in_sems.at[h, g]
        )

    def store(h, p):
        return pltpu.make_async_copy(packed.at[h, p], sent.at[:, p, h], out_sems.at[h, p])

    for h in range(2):
        for g in range(4):
            load(h, g).start()
    for h in range(2):
        for g in range(4):
            load(h, g).wait()
        views = [field.at[h, g].reshape(512, 128) for g in range(4)]
        outs = [packed.at[h, p].reshape(1024, 128) for p in range(2)]
        for group in range(2):
            columns = [
                jnp.concatenate([v[pl.ds(group * 4 + i, 64, stride=8), :] for i in range(4)], axis=0)
                for v in views
            ]
            near, far = side(columns[:2]), side(columns[2:])
            products = [
                table_times_rows(even_left[...], near + far),
                table_times_rows(odd_left[...], near - far),
            ]
            for p in range(2):
                for pair in range(2):
                    lanes = slice(pair * 128, pair * 128 + 128)
                    both = swap_halves(products[p][:128, lanes], products[p][128:, lanes])
                    for i in range(2):
                        z = group * 4 + pair * 2 + i
                        outs[p][pl.ds(z, 128, stride=8), :] = both[i]
        for p in range(2):
            store(h, p).start()
    for h in range(2):
        for p in range(2):
            store(h, p).wait()


def plane_kernel(
    received,
    multipliers,
    z_left,
    even_right,
    odd_right,
    odd_back,
    sent,
    planes,
    spectrum,
    filters,
    filtered,
    fields,
    in_sems,
    filter_sems,
    out_sems,
):
    def load(r, p):
        return pltpu.make_async_copy(received.at[r, :, p], planes.at[r, p], in_sems.at[r, p])

    def load_filter(f, k):
        return pltpu.make_async_copy(multipliers.at[f, k], filters.at[f, k], filter_sems.at[f, k])

    def store(r, f, p):
        return pltpu.make_async_copy(
            fields.at[r, f, p], sent.at[r, :, f, p], out_sems.at[r, f, p]
        )

    for r in range(8):
        for p in range(2):
            load(r, p).start()
    for k in range(4):
        for f in range(2):
            load_filter(f, k).start()
    for r in range(8):
        for p in range(2):
            load(r, p).wait()
        plane = side([planes[r, p].reshape(256, 128) for p in range(2)])
        spectrum[r] = table_times(z_left[...], plane)
    for p in range(2):
        lanes = slice(p * 128, p * 128 + 128)
        columns = [[], []]
        for r in range(0, 8, 2):
            both = swap_halves(spectrum[r, :, lanes], spectrum[r + 1, :, lanes])
            for i in range(2):
                columns[i].append(both[i])
        backs = [[], []]
        for i in range(2):
            k = p * 2 + i
            near, far = side(columns[i][:2]), side(columns[i][2:])
            even = times_table(near + far, even_right[...])
            odd = times_table(near - far, odd_right[...])
            for f in range(2):
                load_filter(f, k).wait()
                back_even = times_table(even * filters[f, k, :, :256], even_right[...])
                back_odd = times_table(odd * filters[f, k, :, 256:], odd_back[...])
                backs[f].append(side([back_even + back_odd, back_even - back_odd]))
        for f in range(2):
            for r in range(0, 8, 2):
                part = slice(r * 64, r * 64 + 128)
                both = swap_halves(backs[f][0][:, part], backs[f][1][:, part])
                for i in range(2):
                    filtered[f, r + i, :, lanes] = both[i]
    for r in range(8):
        for f in range(2):
            field = table_times(z_left[...], filtered[f, r])
            for p in range(2):
                fields[r, f, p] = field[:, p * 128 : p * 128 + 128].reshape(16, 16, 128)
                store(r, f, p).start()
    for r in range(8):
        for f in range(2):
            for p in range(2):
                store(r, f, p).wait()


def update_kernel(
    received,
    even_right,
    odd_back,
    pressure,
    pressure_prior,
    lossy_prior,
    stiffness,
    compensation,
    snapshot,
    image_prior,
    pressure_next,
    lossy_term,
    image_sum,
    parts,
    terms,
    inputs,
    outputs,
    part_sems,
    in_sems,
    out_sems,
):
    sources = (
        pressure, pressure_prior, lossy_prior, stiffness, compensation, snapshot, image_prior
    )
    targets = (pressure_next, lossy_term, image_sum)

    def load_part(h, f, p):
        return pltpu.make_async_copy(received.at[:, f, p, h], parts.at[h, f, p], part_sems.at[h, f, p])

    def load(h, a):
        return pltpu.make_async_copy(sources[a].at[:, h], inputs.at[h, a], in_sems.at[h, a])

    def store(h, a):
        return pltpu.make_async_copy(outputs.at[h, a], targets[a].at[:, h], out_sems.at[h, a])

    for h in range(2):
        for f in range(2):
            for p in range(2):
                load_part(h, f, p).start()
        for a in range(7):
            load(h, a).start()
    for h in range(2):
        for f in range(2):
            for p in range(2):
                load_part(h, f, p).wait()
            views = [parts.at[h, f, p].reshape(1024, 128) for p in range(2)]
            for group in range(2):
                rows = [[], []]
                for i in range(4):
                    for p in range(2):
                        block = views[p][pl.ds(group * 4 + i, 128, stride=8), :].T
                        rows[p].append(side([block[:64], block[64:]]))
                even = times_table(jnp.concatenate(rows[0], axis=0), even_right[...])
                odd = times_table(jnp.concatenate(rows[1], axis=0), odd_back[...])
                both = side([even + odd, even - odd])
                for g in range(4):
                    for i in range(4):
                        terms[f, g, pl.ds(group * 4 + i, 64, stride=8), :] = both[
                            i * 64 : i * 64 + 64, g * 128 : g * 128 + 128
                        ]
        for a in range(7):
            load(h, a).wait()

        def step(y, carry):
            mine = pl.ds(pl.multiple_of(y * 64, 64), 64)
            there = pl.ds(y * 8, 8)
            stiff = side([terms[0, g, mine, :] for g in range(4)]).reshape(8, 8, 512)
            lossy = side([terms[1, g, mine, :] for g in range(4)]).reshape(8, 8, 512)
            now, prior, loss, stiffs, comp, snap, image = [inputs[h, a, there] for a in range(7)]
            value = 2.0 * now - prior - stiffs * stiff + comp * (lossy - loss)
            outputs[h, 0, there] = value
            outputs[h, 1, there] = lossy
            outputs[h, 2, there] = image + snap * value
            return carry

        lax.fori_loop(0, 8, step, 0)
        for a in range(3):
            store(h, a).start()
    for h in range(2):
        for a in range(3):
            store(h, a).wait()


def call(kernel, operands, blocks, out_shape, scratch):
    anywhere = pl.BlockSpec(memory_space=pl.ANY)
    table = pl.BlockSpec(memory_space=pltpu.VMEM)
    specs = [table if i in blocks else anywhere for i in range(len(operands))]
    return pl.pallas_call(
        kernel,
        in_specs=specs,
        out_specs=jax.tree.map(lambda _: anywhere, out_shape),
        out_shape=out_shape,
        scratch_shapes=scratch,
        compiler_params=pltpu.CompilerParams(vmem_limit_bytes=56 * MIB),
    )(*operands)


def wave_square(indices, length):
    folded = jnp.minimum(indices, length - indices)
    return (2.0 * math.pi / length * folded.astype(jnp.float32)) ** 2


def body(pressure, pressure_prior, lossy_prior, stiffness, compensation, snapshot, image_prior):
    axes = ("row", "col")
    half = np.arange(256)
    even_table = cas(half, half, 256)
    odd_table = cas(2 * half + 1, half, 512)
    even_left, odd_left = left_table(even_table), left_table(odd_table)
    even_right = right_table(even_table)
    odd_right, odd_back = right_table(odd_table.T), right_table(odd_table)
    z_left = even_left
    arrays = [
        a.reshape(64, 2, 8, 512)
        for a in (pressure, pressure_prior, lossy_prior, stiffness, compensation, snapshot, image_prior)
    ]
    f32 = jnp.float32
    dma = pltpu.SemaphoreType.DMA

    sent = call(
        forward_x_kernel,
        (arrays[0], even_left, odd_left),
        (1, 2),
        jax.ShapeDtypeStruct((128, 2, 2, 8, 128), f32),
        [
            pltpu.VMEM((2, 4, 64, 8, 128), f32),
            pltpu.VMEM((2, 2, 128, 8, 128), f32),
            dma((2, 4)),
            dma((2, 2)),
        ],
    )
    received = lax.all_to_all(sent.reshape(128, 32, 128), axes, split_axis=0, concat_axis=0, tiled=True)

    device = lax.axis_index("row") * 16 + lax.axis_index("col")
    part = jnp.arange(4, dtype=jnp.int32)
    index_x = 2 * (part % 2 * 128 + device) + part // 2
    even_indices = 2 * jnp.arange(256, dtype=jnp.int32)
    index_y = jnp.concatenate([even_indices, even_indices + 1])
    index_z = jnp.arange(256, dtype=jnp.int32)
    squared = (
        wave_square(index_y, 512)[None, None, :]
        + wave_square(index_z, 256)[None, :, None]
        + wave_square(index_x, 512)[:, None, None]
    )
    normalizer = 1.0 / (512 * 256 * 512)
    multipliers = jnp.stack(
        [
            squared**stiff_power * normalizer,
            squared**lossy_power * jnp.exp(-filter_rate * squared) * normalizer,
        ]
    )

    sent = call(
        plane_kernel,
        (received.reshape(8, 16, 2, 16, 128), multipliers, z_left, even_right, odd_right, odd_back),
        (2, 3, 4, 5),
        jax.ShapeDtypeStruct((8, 16, 2, 2, 16, 128), f32),
        [
            pltpu.VMEM((8, 2, 16, 16, 128), f32),
            pltpu.VMEM((8, 256, 256), f32),
            pltpu.VMEM((2, 4, 256, 512), f32),
            pltpu.VMEM((2, 8, 256, 256), f32),
            pltpu.VMEM((8, 2, 2, 16, 16, 128), f32),
            dma((8, 2)),
            dma((2, 4)),
            dma((8, 2, 2)),
        ],
    )
    received = lax.all_to_all(sent.reshape(128, 64, 128), axes, split_axis=0, concat_axis=0, tiled=True)

    outs = call(
        update_kernel,
        (received.reshape(128, 2, 2, 2, 8, 128), even_right, odd_back, *arrays),
        (1, 2),
        [jax.ShapeDtypeStruct((64, 2, 8, 512), f32)] * 3,
        [
            pltpu.VMEM((2, 2, 2, 128, 8, 128), f32),
            pltpu.VMEM((2, 4, 512, 128), f32),
            pltpu.VMEM((2, 7, 64, 8, 512), f32),
            pltpu.VMEM((2, 3, 64, 8, 512), f32),
            dma((2, 2, 2)),
            dma((2, 7)),
            dma((2, 3)),
        ],
    )
    return tuple(o.reshape(64, 16, 512) for o in outs)


def solution(mesh):
    spec = P("row", "col", None)
    return jax.shard_map(
        body, mesh=mesh, in_specs=(spec,) * 7, out_specs=(spec,) * 3, check_vma=False
    )
```

```python
import functools
import math

import jax
import jax.numpy as jnp
import ml_dtypes
import numpy as np
from jax import lax
from jax.experimental import pallas as pl
from jax.experimental.pallas import tpu as pltpu
from jax.sharding import PartitionSpec as P

stiff_power = 1.03
lossy_power = 0.53
filter_rate = 0.14
MIB = 1 << 20


def split_table(table):
    high = table.astype(ml_dtypes.bfloat16)
    low = (table - high.astype(np.float64)).astype(ml_dtypes.bfloat16)
    return high, low


def cas(left, right, length):
    angle = 2.0 * math.pi / length * (np.outer(left, right) % length)
    return np.cos(angle) + np.sin(angle)


def pieces(values):
    high = values.astype(jnp.bfloat16)
    low = (values - high.astype(jnp.float32)).astype(jnp.bfloat16)
    return high, low


EVEN, ODD = 0, 2


def cat3(high, low, axis):
    return jnp.concatenate([high, low, high], axis=axis)


def product(left, right, right_dim):
    return lax.dot_general(
        left, right, (((1,), (right_dim,)), ((), ())), preferred_element_type=jnp.float32
    )


def times_table(values, tables, which, transposed=False):
    axis = 1 if transposed else 0
    high, low = tables[which], tables[which + 1]
    table = jnp.concatenate([high, high, low], axis=axis)
    return product(cat3(*pieces(values), 1), table, axis)


def table_times(tables, which, values, transposed=False):
    axis = 1 if transposed else 0
    high, low = tables[which], tables[which + 1]
    table = jnp.concatenate([high, high, low], axis=1)
    return product(table, cat3(*pieces(values), axis), axis)


def loop(count, step):
    for i in range(count):
        step(i, 0)


def swap_halves(first, second):
    lane = lax.broadcasted_iota(jnp.int32, first.shape, 1)
    left = jnp.where(lane < 64, first, pltpu.roll(second, 64, 1))
    right = jnp.where(lane < 64, pltpu.roll(first, 64, 1), second)
    return left, right


def side(parts):
    return jnp.concatenate(parts, axis=1)


def forward_x_kernel(pressure, tables, sent, field, packed, table, in_sems, out_sems, table_sem):
    def load(h, g):
        return pltpu.make_async_copy(
            pressure.at[:, h, :, pl.ds(g * 128, 128)], field.at[h, g], in_sems.at[h, g]
        )

    def store(h, p):
        return pltpu.make_async_copy(packed.at[h, p], sent.at[:, p, h], out_sems.at[h, p])

    load_table = pltpu.make_async_copy(tables, table, table_sem)
    for g in range(4):
        load(0, g).start()
    load_table.start()
    for g in range(4):
        load(1, g).start()
    for h in range(2):
        for g in range(4):
            load(h, g).wait()
        if h == 0:
            load_table.wait()
        views = [field.at[h, g].reshape(512, 128) for g in range(4)]
        for p in range(2):
            target = packed.at[h, p].reshape(1024, 128)
            for group in range(2):
                near, far = [
                    side(
                        [
                            jnp.concatenate(
                                [v[pl.ds(group * 4 + i, 64, stride=8), :] for i in range(4)], axis=0
                            )
                            for v in views[half * 2 : half * 2 + 2]
                        ]
                    )
                    for half in range(2)
                ]
                if p == 0:
                    result = times_table(near + far, table, EVEN)
                else:
                    result = times_table(near - far, table, ODD, True)
                for i in range(4):
                    rows = result[i * 64 : i * 64 + 64]
                    block = jnp.concatenate([rows[:, :128], rows[:, 128:]], axis=0)
                    target[pl.ds(group * 4 + i, 128, stride=8), :] = block.T
            store(h, p).start()
    for h in range(2):
        for p in range(2):
            store(h, p).wait()


def plane_kernel(
    received,
    stiff_filter,
    lossy_filter,
    tables,
    sent,
    spectrum,
    whole,
    filtered,
    filters,
    filter_sems,
):
    def load(f, k):
        source = lossy_filter if f else stiff_filter
        return pltpu.make_async_copy(source.at[k], filters.at[f, k], filter_sems.at[f, k])

    for p in range(2):
        for f in range(2):
            for k in (p * 2, p * 2 + 1):
                load(f, k).start()

    def forward_z(r, carry):
        plane = side([received[r, :, p].reshape(256, 128) for p in range(2)])
        result = table_times(tables, EVEN, plane)
        for p in range(2):
            spectrum[p, r] = result[:, p * 128 : p * 128 + 128]
        return carry

    loop(8, forward_z)

    for p in range(2):
        columns = [[], []]
        for r in range(0, 8, 2):
            both = swap_halves(spectrum[p, r], spectrum[p, r + 1])
            for i in range(2):
                columns[i].append(both[i])
        for i in range(2):
            k = p * 2 + i
            near, far = side(columns[i][:2]), side(columns[i][2:])
            whole[k, :, :256] = times_table(near + far, tables, EVEN)
            whole[k, :, 256:] = times_table(near - far, tables, ODD, True)
    for p in range(2):
        for f in range(2):
            backs = []
            for k in (p * 2, p * 2 + 1):
                load(f, k).wait()
                back_even = times_table(whole[k, :, :256] * filters[f, k, :, :256], tables, EVEN)
                back_odd = times_table(whole[k, :, 256:] * filters[f, k, :, 256:], tables, ODD)
                backs.append(side([back_even + back_odd, back_even - back_odd]))
            for r in range(0, 8, 2):
                part = slice(r * 64, r * 64 + 128)
                both = swap_halves(backs[0][:, part], backs[1][:, part])
                for i in range(2):
                    filtered[f, r + i, p] = both[i]

    def back_z(r, carry):
        for f in range(2):
            field = table_times(tables, EVEN, side([filtered[f, r, p] for p in range(2)]))
            for p in range(2):
                sent[r, :, f, p] = field[:, p * 128 : p * 128 + 128].reshape(16, 16, 128)
        return carry

    loop(8, back_z)


def update_kernel(
    received,
    tables,
    pressure,
    pressure_prior,
    lossy_prior,
    stiffness,
    compensation,
    snapshot,
    image_prior,
    pressure_next,
    lossy_term,
    image_sum,
    terms,
    outputs,
    out_sems,
):
    sources = (
        pressure, pressure_prior, lossy_prior, stiffness, compensation, snapshot, image_prior
    )
    targets = (pressure_next, lossy_term, image_sum)

    def store(h, a, part):
        mine = pl.ds(part * 16, 16)
        return pltpu.make_async_copy(
            outputs.at[h, a, mine], targets[a].at[mine, h], out_sems.at[h, a, part]
        )

    for h in range(2):
        for f in (1, 0):
            for group in range(2):
                rows = [[], []]
                for i in range(4):
                    for p in range(2):
                        place = f * 32 + p * 16 + h * 8 + group * 4 + i
                        block = received[pl.ds(place, 128, stride=64), :].T
                        rows[p].append(side([block[:64], block[64:]]))
                even = times_table(jnp.concatenate(rows[0], axis=0), tables, EVEN)
                odd = times_table(jnp.concatenate(rows[1], axis=0), tables, ODD)
                both = side([even + odd, even - odd])
                for g in range(4):
                    for i in range(4):
                        terms[f, g, pl.ds(group * 4 + i, 64, stride=8), :] = both[
                            i * 64 : i * 64 + 64, g * 128 : g * 128 + 128
                        ]
            if f:
                for part in range(4):
                    for y in range(part * 2, part * 2 + 2):
                        mine = pl.ds(y * 64, 64)
                        lossy = side([terms[1, g, mine, :] for g in range(4)])
                        outputs[h, 1, pl.ds(y * 8, 8)] = lossy.reshape(8, 8, 512)
                    store(h, 1, part).start()
        for part in range(4):
            for y in range(part * 2, part * 2 + 2):
                mine = pl.ds(y * 64, 64)
                there = pl.ds(y * 8, 8)
                stiff = side([terms[0, g, mine, :] for g in range(4)]).reshape(8, 8, 512)
                lossy = outputs[h, 1, there]
                now, prior, loss, stiffs, comp, snap, image = [s[there, h] for s in sources]
                value = 2.0 * now - prior - stiffs * stiff + comp * (lossy - loss)
                outputs[h, 0, there] = value
                outputs[h, 2, there] = image + snap * value
            store(h, 0, part).start()
            store(h, 2, part).start()
    for h in range(2):
        for a in range(3):
            for part in range(4):
                store(h, a, part).wait()


def held(array):
    return pltpu.with_memory_space_constraint(array, pltpu.VMEM)


def outer(array):
    return pltpu.with_memory_space_constraint(array, pltpu.HBM)


def call(kernel, operands, outside, out_shape, scratch, limit):
    anywhere = pl.BlockSpec(memory_space=pl.ANY)
    vmem = pl.BlockSpec(memory_space=pltpu.VMEM)
    return pl.pallas_call(
        kernel,
        in_specs=[anywhere if i in outside else vmem for i in range(len(operands))],
        out_specs=jax.tree.map(
            lambda s: anywhere if isinstance(s, jax.ShapeDtypeStruct) else vmem, out_shape
        ),
        out_shape=out_shape,
        scratch_shapes=scratch,
        compiler_params=pltpu.CompilerParams(vmem_limit_bytes=limit * MIB),
    )(*operands)


def wave_square(indices, length):
    folded = jnp.minimum(indices, length - indices)
    return (2.0 * math.pi / length * folded.astype(jnp.float32)) ** 2


def body(pressure, pressure_prior, lossy_prior, stiffness, compensation, snapshot, image_prior):
    axes = ("row", "col")
    half = np.arange(256)
    even_table = cas(half, half, 256)
    odd_table = cas(2 * half + 1, half, 512)
    tables = np.stack([*split_table(even_table), *split_table(odd_table)])
    arrays = [
        a.reshape(64, 2, 8, 512)
        for a in (pressure, pressure_prior, lossy_prior, stiffness, compensation, snapshot, image_prior)
    ]
    f32 = jnp.float32
    dma = pltpu.SemaphoreType.DMA

    sent = call(
        forward_x_kernel,
        (outer(arrays[0]), outer(tables)),
        (0, 1),
        jax.ShapeDtypeStruct((128, 2, 2, 8, 128), f32),
        [
            pltpu.VMEM((2, 4, 64, 8, 128), f32),
            pltpu.VMEM((2, 2, 128, 8, 128), f32),
            pltpu.VMEM((4, 256, 256), jnp.bfloat16),
            dma((2, 4)),
            dma((2, 2)),
            dma,
        ],
        12,
    )
    received = lax.all_to_all(sent.reshape(128, 32, 128), axes, split_axis=0, concat_axis=0, tiled=True)

    device = lax.axis_index("row") * 16 + lax.axis_index("col")
    part = jnp.arange(4, dtype=jnp.int32)
    index_x = 2 * (part % 2 * 128 + device) + part // 2
    even_indices = 2 * jnp.arange(256, dtype=jnp.int32)
    index_y = jnp.concatenate([even_indices, even_indices + 1])
    index_z = jnp.arange(256, dtype=jnp.int32)
    squared = (
        wave_square(index_y, 512)[None, None, :]
        + wave_square(index_z, 256)[None, :, None]
        + wave_square(index_x, 512)[:, None, None]
    )
    normalizer = 1.0 / (512 * 256 * 512)
    stiff_filter = squared**stiff_power * normalizer
    lossy_filter = squared**lossy_power * jnp.exp(-filter_rate * squared) * normalizer

    sent = call(
        plane_kernel,
        (
            held(received.reshape(8, 16, 2, 16, 128)),
            outer(stiff_filter),
            outer(lossy_filter),
            held(tables),
        ),
        (1, 2),
        pltpu.VMEM((8, 16, 2, 2, 16, 128), f32),
        [
            pltpu.VMEM((2, 8, 256, 128), f32),
            pltpu.VMEM((4, 256, 512), f32),
            pltpu.VMEM((2, 8, 2, 256, 128), f32),
            pltpu.VMEM((2, 4, 256, 512), f32),
            dma((2, 4)),
        ],
        16,
    )
    received = lax.all_to_all(sent.reshape(128, 64, 128), axes, split_axis=0, concat_axis=0, tiled=True)

    outs = call(
        update_kernel,
        (held(received.reshape(8192, 128)), held(tables), *map(held, arrays)),
        (),
        [jax.ShapeDtypeStruct((64, 2, 8, 512), f32)] * 3,
        [
            pltpu.VMEM((2, 4, 512, 128), f32),
            pltpu.VMEM((2, 3, 64, 8, 512), f32),
            dma((2, 3, 4)),
        ],
        16,
    )
    return tuple(o.reshape(64, 16, 512) for o in outs)


def solution(mesh):
    spec = P("row", "col", None)
    return jax.shard_map(
        body, mesh=mesh, in_specs=(spec,) * 7, out_specs=(spec,) * 3, check_vma=False
    )
```

```python
import functools
import math

import jax
import jax.numpy as jnp
import ml_dtypes
import numpy as np
from jax import lax
from jax.experimental import pallas as pl
from jax.experimental.pallas import tpu as pltpu
from jax.sharding import PartitionSpec as P

stiff_power = 1.03
lossy_power = 0.53
filter_rate = 0.14
MIB = 1 << 20


def split_table(table):
    high = table.astype(ml_dtypes.bfloat16)
    low = (table - high.astype(np.float64)).astype(ml_dtypes.bfloat16)
    return high, low


def cas(left, right, length):
    angle = 2.0 * math.pi / length * (np.outer(left, right) % length)
    return np.cos(angle) + np.sin(angle)


def pieces(values):
    high = values.astype(jnp.bfloat16)
    low = (values - high.astype(jnp.float32)).astype(jnp.bfloat16)
    return high, low


EVEN, ODD, EVEN_BACK = 0, 2, 4


def cat3(high, low, axis):
    return jnp.concatenate([high, low, high], axis=axis)


def product(left, right, right_dim):
    return lax.dot_general(
        left, right, (((1,), (right_dim,)), ((), ())), preferred_element_type=jnp.float32
    )


def times_table(values, tables, which, transposed=False):
    axis = 1 if transposed else 0
    high, low = tables[which], tables[which + 1]
    table = jnp.concatenate([high, high, low], axis=axis)
    return product(cat3(*pieces(values), 1), table, axis)


def table_times(tables, which, values, transposed=False):
    axis = 1 if transposed else 0
    high, low = tables[which], tables[which + 1]
    table = jnp.concatenate([high, high, low], axis=1)
    return product(table, cat3(*pieces(values), axis), axis)


def loop(count, step):
    for i in range(count):
        step(i, 0)


def swap_halves(first, second):
    lane = lax.broadcasted_iota(jnp.int32, first.shape, 1)
    left = jnp.where(lane < 64, first, pltpu.roll(second, 64, 1))
    right = jnp.where(lane < 64, pltpu.roll(first, 64, 1), second)
    return left, right


def side(parts):
    return jnp.concatenate(parts, axis=1)


def write_filters(device, filters):
    normalizer = 1.0 / (512 * 256 * 512)
    lane = lax.broadcasted_iota(jnp.int32, (8, 128), 1)
    row = lax.broadcasted_iota(jnp.int32, (8, 128), 0)
    even_y = 2 * lane
    waves_y = [even_y, jnp.where(lane == 0, 256, even_y), even_y + 1]
    even_x = 2 * device
    waves_x = [even_x, jnp.where(device == 0, 256, even_x), even_x + 1]

    def square(wave, length):
        return (2.0 * math.pi / length * wave.astype(jnp.float32)) ** 2

    squares_y = [square(wave, 512) for wave in waves_y]
    squares_x = [square(wave, 512) for wave in waves_x]
    for tile in range(17):
        wave_z = row + tile * 8 if tile < 16 else jnp.where(row == 0, 128, row)
        square_z = square(wave_z, 256)
        for j in range(3):
            square_yz = squares_y[j] + square_z
            for q in range(3):
                squared = square_yz + squares_x[q]
                logarithm = jnp.log(squared)
                place = (q, slice(tile * 8, tile * 8 + 8), slice(j * 128, j * 128 + 128))
                filters[(0, *place)] = jnp.exp(stiff_power * logarithm) * normalizer
                filters[(1, *place)] = (
                    jnp.exp(lossy_power * logarithm - filter_rate * squared) * normalizer
                )


def forward_x_kernel(device, pressure, tables, sent, filters, field, table, in_sems, table_sem):
    def load(h, g):
        return pltpu.make_async_copy(
            pressure.at[:, h, :, pl.ds(g * 128, 128)], field.at[h, g], in_sems.at[h, g]
        )

    load_table = pltpu.make_async_copy(tables.at[pl.ds(0, 4)], table, table_sem)
    for g in range(4):
        load(0, g).start()
    load_table.start()
    for g in range(4):
        load(1, g).start()
    write_filters(device[0], filters)
    load_table.wait()
    for h in range(2):
        for g in range(4):
            load(h, g).wait()
        views = [field.at[h, g].reshape(512, 128) for g in range(4)]
        for group in range(2):
            near, far = [
                side(
                    [
                        jnp.concatenate(
                            [v[pl.ds(group * 4 + i, 64, stride=8), :] for i in range(4)], axis=0
                        )
                        for v in views[half * 2 : half * 2 + 2]
                    ]
                )
                for half in range(2)
            ]
            results = [
                times_table(near + far, table, EVEN),
                times_table(near - far, table, ODD, True),
            ]
            for p in range(2):
                for i in range(4):
                    rows = results[p][i * 64 : i * 64 + 64]
                    block = jnp.concatenate([rows[:, :128], rows[:, 128:]], axis=0)
                    place = p * 16 + h * 8 + group * 4 + i
                    sent[pl.ds(place, 128, stride=32), :] = block.T


def plane_kernel(received, filters, tables, sent, spectrum, whole, filtered):
    chunks = [(high, x, core) for x in range(4) for high in range(2) for core in range(2)]
    for r in range(8):
        low, y = divmod(r, 4)
        plane = jnp.concatenate(
            [
                side([received[high, low, y, x, core, p] for p in range(2)])
                for high, x, core in chunks
            ],
            axis=0,
        )
        result = table_times(tables, EVEN_BACK, plane)
        for p in range(2):
            spectrum[p, r] = result[:, p * 128 : p * 128 + 128]
    for p in range(2):
        columns = [[], []]
        for r in range(0, 8, 2):
            both = swap_halves(spectrum[p, r], spectrum[p, r + 1])
            for i in range(2):
                columns[i].append(both[i])
        for i in range(2):
            k = p * 2 + i
            near, far = side(columns[i][:2]), side(columns[i][2:])
            whole[k, :, :256] = times_table(near + far, tables, EVEN)
            whole[k, :, 256:] = times_table(near - far, tables, ODD, True)
    for p in range(2):
        for f in range(2):
            backs = []
            for k in (p * 2, p * 2 + 1):
                q = min(k, 2)
                filter_rows = jnp.concatenate(
                    [filters[f, q, 0:128], filters[f, q, 128:136], filters[f, q, 8:128]], axis=0
                )
                filter_odd = side([filter_rows[:, 256:], filter_rows[:, 256:]])
                back_even = times_table(whole[k, :, :256] * filter_rows[:, :256], tables, EVEN_BACK)
                back_odd = times_table(whole[k, :, 256:] * filter_odd, tables, ODD)
                backs.append(side([back_even + back_odd, back_even - back_odd]))
            for r in range(0, 8, 2):
                part = slice(r * 64, r * 64 + 128)
                both = swap_halves(backs[0][:, part], backs[1][:, part])
                for i in range(2):
                    filtered[f, r + i, p] = both[i]
    for r in range(8):
        low, y = divmod(r, 4)
        for f in range(2):
            field = table_times(tables, EVEN, side([filtered[f, r, p] for p in range(2)]))
            for c, (high, x, core) in enumerate(chunks):
                for p in range(2):
                    sent[high, low, y, x, core, f, p] = field[
                        c * 16 : c * 16 + 16, p * 128 : p * 128 + 128
                    ]


def update_kernel(
    received,
    tables,
    pressure,
    pressure_prior,
    lossy_prior,
    stiffness,
    compensation,
    snapshot,
    image_prior,
    pressure_next,
    lossy_term,
    image_sum,
    terms,
    outputs,
    out_sems,
):
    sources = (
        pressure, pressure_prior, lossy_prior, stiffness, compensation, snapshot, image_prior
    )
    targets = (pressure_next, lossy_term, image_sum)

    def store(h, a, part):
        mine = pl.ds(part * 16, 16)
        return pltpu.make_async_copy(
            outputs.at[h, a, mine], targets[a].at[mine, h], out_sems.at[h, a, part]
        )

    for h in range(2):
        for f in (1, 0):
            for group in range(2):
                rows = [[], []]
                for i in range(4):
                    for p in range(2):
                        place = f * 32 + p * 16 + h * 8 + group * 4 + i
                        block = received[pl.ds(place, 128, stride=64), :].T
                        rows[p].append(side([block[:64], block[64:]]))
                even = times_table(jnp.concatenate(rows[0], axis=0), tables, EVEN_BACK)
                odd = times_table(jnp.concatenate(rows[1], axis=0), tables, ODD)
                both = side([even + odd, even - odd])
                for g in range(4):
                    for i in range(4):
                        terms[f, g, pl.ds(group * 4 + i, 64, stride=8), :] = both[
                            i * 64 : i * 64 + 64, g * 128 : g * 128 + 128
                        ]
            if f:
                for part in range(4):
                    for y in range(part * 2, part * 2 + 2):
                        mine = pl.ds(y * 64, 64)
                        lossy = side([terms[1, g, mine, :] for g in range(4)])
                        outputs[h, 1, pl.ds(y * 8, 8)] = lossy.reshape(8, 8, 512)
                    store(h, 1, part).start()
        for part in range(4):
            for y in range(part * 2, part * 2 + 2):
                mine = pl.ds(y * 64, 64)
                there = pl.ds(y * 8, 8)
                stiff = side([terms[0, g, mine, :] for g in range(4)]).reshape(8, 8, 512)
                lossy = outputs[h, 1, there]
                now, prior, loss, stiffs, comp, snap, image = [s[there, h] for s in sources]
                value = 2.0 * now - prior - stiffs * stiff + comp * (lossy - loss)
                outputs[h, 0, there] = value
                outputs[h, 2, there] = image + snap * value
            store(h, 0, part).start()
            store(h, 2, part).start()
    for h in range(2):
        for a in range(3):
            for part in range(4):
                store(h, a, part).wait()


def held(array):
    return pltpu.with_memory_space_constraint(array, pltpu.VMEM)


def outer(array):
    return pltpu.with_memory_space_constraint(array, pltpu.HBM)


def call(kernel, operands, spaces, out_shape, scratch, limit):
    return pl.pallas_call(
        kernel,
        in_specs=[pl.BlockSpec(memory_space=space) for space in spaces],
        out_specs=[
            pl.BlockSpec(memory_space=pl.ANY if isinstance(s, jax.ShapeDtypeStruct) else pltpu.VMEM)
            for s in out_shape
        ],
        out_shape=out_shape,
        scratch_shapes=scratch,
        compiler_params=pltpu.CompilerParams(vmem_limit_bytes=limit * MIB),
    )(*operands)


def exchange(array, order):
    return lax.all_to_all(
        array, ("row", "col"), split_axis=0, concat_axis=0, tiled=True, axis_index_groups=[order]
    )


def body(pressure, pressure_prior, lossy_prior, stiffness, compensation, snapshot, image_prior):
    half = np.arange(256)
    even_order = np.concatenate([half[:128], [128], half[:128:-1]])
    odd_order = np.concatenate([half[:128], half[:127:-1]])
    even_table = cas(half, even_order, 256)
    odd_table = cas(2 * odd_order + 1, half, 512)
    tables = np.stack(
        [*split_table(even_table), *split_table(odd_table), *split_table(even_table.T)]
    )
    place = np.arange(128).reshape(2, 4, 4, 2, 2)
    order = [int(i) for i in place.transpose(3, 0, 1, 2, 4).reshape(-1)]
    row, col = lax.axis_index("row"), lax.axis_index("col")
    device = (col // 2 % 2 * 2 + row // 4) * 32 + row % 4 * 8 + col // 4 * 2 + col % 2
    arrays = [
        a.reshape(64, 2, 8, 512)
        for a in (pressure, pressure_prior, lossy_prior, stiffness, compensation, snapshot, image_prior)
    ]
    f32 = jnp.float32
    dma = pltpu.SemaphoreType.DMA
    vmem = pltpu.VMEM

    sent, filters = call(
        forward_x_kernel,
        (device.reshape(1), outer(arrays[0]), outer(tables)),
        (pltpu.SMEM, pl.ANY, pl.ANY),
        [vmem((4096, 128), f32), vmem((2, 3, 136, 384), f32)],
        [
            vmem((2, 4, 64, 8, 128), f32),
            vmem((4, 256, 256), jnp.bfloat16),
            dma((2, 4)),
            dma,
        ],
        12,
    )
    received = exchange(sent.reshape(128, 32, 128), order)

    (sent,) = call(
        plane_kernel,
        (held(received.reshape(2, 2, 4, 4, 2, 2, 16, 128)), held(filters), held(tables)),
        (vmem, vmem, vmem),
        [vmem((2, 2, 4, 4, 2, 2, 2, 16, 128), f32)],
        [
            vmem((2, 8, 256, 128), f32),
            vmem((4, 256, 512), f32),
            vmem((2, 8, 2, 256, 128), f32),
        ],
        16,
    )
    received = exchange(sent.reshape(128, 64, 128), order)

    outs = call(
        update_kernel,
        (held(received.reshape(8192, 128)), held(tables), *map(held, arrays)),
        (vmem,) * 9,
        [jax.ShapeDtypeStruct((64, 2, 8, 512), f32)] * 3,
        [
            vmem((2, 4, 512, 128), f32),
            vmem((2, 3, 64, 8, 512), f32),
            dma((2, 3, 4)),
        ],
        16,
    )
    return tuple(o.reshape(64, 16, 512) for o in outs)


def solution(mesh):
    spec = P("row", "col", None)
    return jax.shard_map(
        body, mesh=mesh, in_specs=(spec,) * 7, out_specs=(spec,) * 3, check_vma=False
    )
```

```python
import functools
import math

import jax
import jax.numpy as jnp
import ml_dtypes
import numpy as np
from jax import lax
from jax.experimental import pallas as pl
from jax.experimental.pallas import tpu as pltpu
from jax.sharding import PartitionSpec as P

stiff_power = 1.03
lossy_power = 0.53
filter_rate = 0.14
MIB = 1 << 20


def split_table(table):
    high = table.astype(ml_dtypes.bfloat16)
    low = (table - high.astype(np.float64)).astype(ml_dtypes.bfloat16)
    return high, low


def cas(left, right, length):
    angle = 2.0 * math.pi / length * (np.outer(left, right) % length)
    return np.cos(angle) + np.sin(angle)


def pieces(values):
    high = values.astype(jnp.bfloat16)
    low = (values - high.astype(jnp.float32)).astype(jnp.bfloat16)
    return high, low


EVEN, ODD, EVEN_BACK = 0, 2, 4
PARTS = (1, 3)


def cat3(high, low, axis):
    return jnp.concatenate([high, low, high], axis=axis)


def product(left, right, right_dim):
    return lax.dot_general(
        left, right, (((1,), (right_dim,)), ((), ())), preferred_element_type=jnp.float32
    )


def times_table(values, tables, which, transposed=False):
    axis = 1 if transposed else 0
    high, low = tables[which], tables[which + 1]
    table = jnp.concatenate([high, high, low], axis=axis)
    return product(cat3(*pieces(values), 1), table, axis)


def table_times(tables, which, values, transposed=False):
    axis = 1 if transposed else 0
    high, low = tables[which], tables[which + 1]
    table = jnp.concatenate([high, high, low], axis=1)
    return product(table, cat3(*pieces(values), axis), axis)


def loop(count, step):
    for i in range(count):
        step(i, 0)


def swap_halves(first, second):
    lane = lax.broadcasted_iota(jnp.int32, first.shape, 1)
    left = jnp.where(lane < 64, first, pltpu.roll(second, 64, 1))
    right = jnp.where(lane < 64, pltpu.roll(first, 64, 1), second)
    return left, right


def side(parts):
    return jnp.concatenate(parts, axis=1)


def write_filters(device, filters):
    normalizer = 1.0 / (512 * 256 * 512)
    lane = lax.broadcasted_iota(jnp.int32, (8, 128), 1)
    row = lax.broadcasted_iota(jnp.int32, (8, 128), 0)
    even_y = 2 * lane
    waves_y = [even_y, jnp.where(lane == 0, 256, even_y), even_y + 1]
    even_x = 2 * device
    waves_x = [even_x, jnp.where(device == 0, 256, even_x), even_x + 1]

    def square(wave, length):
        return (2.0 * math.pi / length * wave.astype(jnp.float32)) ** 2

    squares_y = [square(wave, 512) for wave in waves_y]
    squares_x = [square(wave, 512) for wave in waves_x]
    for tile in range(17):
        wave_z = row + tile * 8 if tile < 16 else jnp.where(row == 0, 128, row)
        square_z = square(wave_z, 256)
        for j in range(3):
            square_yz = squares_y[j] + square_z
            for q in range(3):
                squared = square_yz + squares_x[q]
                logarithm = jnp.log(squared)
                place = (q, slice(tile * 8, tile * 8 + 8), slice(j * 128, j * 128 + 128))
                filters[(0, *place)] = jnp.exp(stiff_power * logarithm) * normalizer
                filters[(1, *place)] = (
                    jnp.exp(lossy_power * logarithm - filter_rate * squared) * normalizer
                )


def forward_x_kernel(device, pressure, tables, sent, filters, field, table, in_sems, table_sem):
    def load(h, g):
        return pltpu.make_async_copy(
            pressure.at[:, h, :, pl.ds(g * 128, 128)], field.at[h, g], in_sems.at[h, g]
        )

    load_table = pltpu.make_async_copy(tables.at[pl.ds(0, 4)], table, table_sem)
    for g in range(4):
        load(0, g).start()
    load_table.start()
    for g in range(4):
        load(1, g).start()
    write_filters(device[0], filters)
    load_table.wait()
    for h in range(2):
        for g in range(4):
            load(h, g).wait()
        views = [field.at[h, g].reshape(512, 128) for g in range(4)]
        blocks = [[], []]
        for group in range(2):
            near, far = [
                side(
                    [
                        jnp.concatenate(
                            [v[pl.ds(group * 4 + i, 64, stride=8), :] for i in range(4)], axis=0
                        )
                        for v in views[half * 2 : half * 2 + 2]
                    ]
                )
                for half in range(2)
            ]
            results = [
                times_table(near + far, table, EVEN),
                times_table(near - far, table, ODD, True),
            ]
            for p in range(2):
                for i in range(4):
                    rows = results[p][i * 64 : i * 64 + 64]
                    block = jnp.concatenate([rows[:, :128], rows[:, 128:]], axis=0)
                    blocks[p].append(block.T)
        for p in range(2):
            sent[:, p, h] = jnp.swapaxes(jnp.stack(blocks[p], axis=0), 0, 1)


def plane_kernel(received, filters, tables, sent, spectrum, whole, filtered):
    chunks = [(high, x, core) for x in range(4) for high in range(2) for core in range(2)]
    for r in range(8):
        low, y = divmod(r, 4)
        plane = jnp.concatenate(
            [
                side([received[high, low, y, x, core, p] for p in range(2)])
                for high, x, core in chunks
            ],
            axis=0,
        )
        result = table_times(tables, EVEN_BACK, plane)
        for p in range(2):
            spectrum[p, r] = result[:, p * 128 : p * 128 + 128]
    for p in range(2):
        columns = [[], []]
        for r in range(0, 8, 2):
            both = swap_halves(spectrum[p, r], spectrum[p, r + 1])
            for i in range(2):
                columns[i].append(both[i])
        for i in range(2):
            k = p * 2 + i
            near, far = side(columns[i][:2]), side(columns[i][2:])
            whole[k, :, :256] = times_table(near + far, tables, EVEN)
            whole[k, :, 256:] = times_table(near - far, tables, ODD, True)
    for p in range(2):
        for f in range(2):
            backs = []
            for k in (p * 2, p * 2 + 1):
                q = min(k, 2)
                filter_rows = jnp.concatenate(
                    [filters[f, q, 0:128], filters[f, q, 128:136], filters[f, q, 8:128]], axis=0
                )
                filter_odd = side([filter_rows[:, 256:], filter_rows[:, 256:]])
                back_even = times_table(whole[k, :, :256] * filter_rows[:, :256], tables, EVEN_BACK)
                back_odd = times_table(whole[k, :, 256:] * filter_odd, tables, ODD)
                backs.append(side([back_even + back_odd, back_even - back_odd]))
            for r in range(0, 8, 2):
                part = slice(r * 64, r * 64 + 128)
                both = swap_halves(backs[0][:, part], backs[1][:, part])
                for i in range(2):
                    filtered[f, r + i, p] = both[i]
    for r in range(8):
        low, y = divmod(r, 4)
        for f in range(2):
            field = table_times(tables, EVEN, side([filtered[f, r, p] for p in range(2)]))
            for c, (high, x, core) in enumerate(chunks):
                for p in range(2):
                    sent[high, low, y, x, core, f, p] = field[
                        c * 16 : c * 16 + 16, p * 128 : p * 128 + 128
                    ]


def update_kernel(
    received,
    tables,
    pressure,
    pressure_prior,
    lossy_prior,
    stiffness,
    compensation,
    snapshot,
    image_prior,
    pressure_next,
    lossy_term,
    image_sum,
    terms,
    outputs,
    out_sems,
):
    sources = (
        pressure, pressure_prior, lossy_prior, stiffness, compensation, snapshot, image_prior
    )
    targets = (pressure_next, lossy_term, image_sum)

    def store(h, a, part):
        if a == 1:
            lanes = pl.ds(part * 128, 128)
            return pltpu.make_async_copy(
                terms.at[h, 1, part], targets[1].at[:, h, :, lanes], out_sems.at[h, 1, part]
            )
        mine = pl.ds((part - 1) * 16, 32)
        return pltpu.make_async_copy(
            outputs.at[h, a // 2, mine], targets[a].at[mine, h], out_sems.at[h, a, part]
        )

    def back_x(h, f):
        fields = [jnp.swapaxes(received[:, f, p, h], 0, 1) for p in range(2)]
        for group in range(2):
            rows = [[], []]
            for i in range(4):
                for p in range(2):
                    block = fields[p][group * 4 + i].T
                    rows[p].append(side([block[:64], block[64:]]))
            even = times_table(jnp.concatenate(rows[0], axis=0), tables, EVEN_BACK)
            odd = times_table(jnp.concatenate(rows[1], axis=0), tables, ODD)
            both = side([even + odd, even - odd])
            for g in range(4):
                view = terms.at[h, f, g].reshape(512, 128)
                for i in range(4):
                    view[pl.ds(group * 4 + i, 64, stride=8), :] = both[
                        i * 64 : i * 64 + 64, g * 128 : g * 128 + 128
                    ]

    for h in range(2):
        back_x(h, 1)
        for part in range(4):
            store(h, 1, part).start()
    for h in range(2):
        back_x(h, 0)
        for part in range(4):
            for y in range(part * 16, part * 16 + 16, 8):
                there = pl.ds(y, 8)
                stiff, lossy = [
                    jnp.concatenate([terms[h, f, g, there] for g in range(4)], axis=2)
                    for f in range(2)
                ]
                now, prior, loss, stiffs, comp, snap, image = [s[there, h] for s in sources]
                value = 2.0 * now - prior - stiffs * stiff + comp * (lossy - loss)
                outputs[h, 0, there] = value
                outputs[h, 1, there] = image + snap * value
            if part in PARTS:
                for a in (0, 2):
                    store(h, a, part).start()
    for h in range(2):
        for a in range(3):
            for part in (range(4) if a == 1 else PARTS):
                store(h, a, part).wait()


def held(array):
    return pltpu.with_memory_space_constraint(array, pltpu.VMEM)


def outer(array):
    return pltpu.with_memory_space_constraint(array, pltpu.HBM)


def call(kernel, operands, spaces, out_shape, scratch, limit):
    return pl.pallas_call(
        kernel,
        in_specs=[pl.BlockSpec(memory_space=space) for space in spaces],
        out_specs=[
            pl.BlockSpec(memory_space=pl.ANY if isinstance(s, jax.ShapeDtypeStruct) else pltpu.VMEM)
            for s in out_shape
        ],
        out_shape=out_shape,
        scratch_shapes=scratch,
        compiler_params=pltpu.CompilerParams(vmem_limit_bytes=limit * MIB),
    )(*operands)


def exchange(array, order):
    return lax.all_to_all(
        array, ("row", "col"), split_axis=0, concat_axis=0, tiled=True, axis_index_groups=[order]
    )


def body(pressure, pressure_prior, lossy_prior, stiffness, compensation, snapshot, image_prior):
    half = np.arange(256)
    even_order = np.concatenate([half[:128], [128], half[:128:-1]])
    odd_order = np.concatenate([half[:128], half[:127:-1]])
    even_table = cas(half, even_order, 256)
    odd_table = cas(2 * odd_order + 1, half, 512)
    tables = np.stack(
        [*split_table(even_table), *split_table(odd_table), *split_table(even_table.T)]
    )
    place = np.arange(128).reshape(2, 4, 4, 2, 2)
    order = [int(i) for i in place.transpose(3, 0, 1, 2, 4).reshape(-1)]
    row, col = lax.axis_index("row"), lax.axis_index("col")
    device = (col // 2 % 2 * 2 + row // 4) * 32 + row % 4 * 8 + col // 4 * 2 + col % 2
    arrays = [
        a.reshape(64, 2, 8, 512)
        for a in (pressure, pressure_prior, lossy_prior, stiffness, compensation, snapshot, image_prior)
    ]
    f32 = jnp.float32
    dma = pltpu.SemaphoreType.DMA
    vmem = pltpu.VMEM

    sent, filters = call(
        forward_x_kernel,
        (device.reshape(1), outer(arrays[0]), outer(tables)),
        (pltpu.SMEM, pl.ANY, pl.ANY),
        [vmem((128, 2, 2, 8, 128), f32), vmem((2, 3, 136, 384), f32)],
        [
            vmem((2, 4, 64, 8, 128), f32),
            vmem((4, 256, 256), jnp.bfloat16),
            dma((2, 4)),
            dma,
        ],
        12,
    )
    received = exchange(sent.reshape(128, 32, 128), order)

    (sent,) = call(
        plane_kernel,
        (held(received.reshape(2, 2, 4, 4, 2, 2, 16, 128)), held(filters), held(tables)),
        (vmem, vmem, vmem),
        [vmem((2, 2, 4, 4, 2, 2, 2, 16, 128), f32)],
        [
            vmem((2, 8, 256, 128), f32),
            vmem((4, 256, 512), f32),
            vmem((2, 8, 2, 256, 128), f32),
        ],
        16,
    )
    received = exchange(sent.reshape(128, 64, 128), order)

    outs = call(
        update_kernel,
        (held(received.reshape(128, 2, 2, 2, 8, 128)), held(tables), *map(held, arrays)),
        (vmem,) * 9,
        [jax.ShapeDtypeStruct((64, 2, 8, 512), f32)] * 3,
        [
            vmem((2, 2, 4, 64, 8, 128), f32),
            vmem((2, 2, 64, 8, 512), f32),
            dma((2, 3, 4)),
        ],
        16,
    )
    return tuple(o.reshape(64, 16, 512) for o in outs)


def solution(mesh):
    spec = P("row", "col", None)
    return jax.shard_map(
        body, mesh=mesh, in_specs=(spec,) * 7, out_specs=(spec,) * 3, check_vma=False
    )
```

```python
import functools
import math

import jax
import jax.numpy as jnp
import ml_dtypes
import numpy as np
from jax import lax
from jax.experimental import pallas as pl
from jax.experimental.pallas import tpu as pltpu
from jax.sharding import PartitionSpec as P

stiff_power = 1.03
lossy_power = 0.53
filter_rate = 0.14
MIB = 1 << 20


def split_table(table):
    high = table.astype(ml_dtypes.bfloat16)
    low = (table - high.astype(np.float64)).astype(ml_dtypes.bfloat16)
    return high, low


def cas(left, right, length):
    angle = 2.0 * math.pi / length * (np.outer(left, right) % length)
    return np.cos(angle) + np.sin(angle)


def block_table(table):
    high, low = split_table(table)
    return np.block([[high, high], [low, np.zeros_like(low)]])


def pieces(values):
    high = values.astype(jnp.bfloat16)
    low = (values - high.astype(jnp.float32)).astype(jnp.bfloat16)
    return high, low


SPLIT, ODD, SPLIT_BACK = (0, 1), 2, (4, 5)
PARTS = (1, 3)


def product(left, right, right_dim):
    return lax.dot_general(
        left, right, (((1,), (right_dim,)), ((), ())), preferred_element_type=jnp.float32
    )


def times_odd(values, tables, transposed):
    axis = 1 if transposed else 0
    high, low = pieces(values)
    table = jnp.concatenate([tables[ODD], tables[ODD], tables[ODD + 1]], axis=axis)
    return product(jnp.concatenate([high, low, high], axis=1), table, axis)


def times_block(values, table):
    both = product(jnp.concatenate(pieces(values), axis=1), table, 1)
    return both[:, :128] + both[:, 128:]


def block_times(table, values):
    both = product(table, jnp.concatenate(pieces(values), axis=0), 0)
    return both[:128] + both[128:]


def even_forward(values, tables):
    near, far = values[:, :128], values[:, 128:]
    return side([times_block(near + far, tables[SPLIT[0]]), times_block(near - far, tables[SPLIT[1]])])


def even_back(values, tables):
    even = times_block(values[:, :128], tables[SPLIT_BACK[0]])
    odd = times_block(values[:, 128:], tables[SPLIT_BACK[1]])
    return side([even + odd, even - odd])


def swap_halves(first, second):
    lane = lax.broadcasted_iota(jnp.int32, first.shape, 1)
    left = jnp.where(lane < 64, first, pltpu.roll(second, 64, 1))
    right = jnp.where(lane < 64, pltpu.roll(first, 64, 1), second)
    return left, right


def side(parts):
    return jnp.concatenate(parts, axis=1)


def write_filters(device, filters):
    normalizer = 1.0 / (512 * 256 * 512)
    lane = lax.broadcasted_iota(jnp.int32, (8, 128), 1)
    row = lax.broadcasted_iota(jnp.int32, (8, 128), 0)

    def waves(place):
        fourth = 4 * (place % 64)
        return [jnp.where(place == 64, 256, fourth), fourth + 2, 2 * place + 1]

    waves_y, waves_x = waves(lane), waves(device)

    def square(wave, length):
        return (2.0 * math.pi / length * wave.astype(jnp.float32)) ** 2

    squares_y = [square(wave, 512) for wave in waves_y]
    squares_x = [square(wave, 512) for wave in waves_x]
    for tile in range(17):
        wave_z = 2 * (row + tile % 8 * 8) + tile // 8 if tile < 16 else jnp.where(row == 0, 128, 2 * row)
        square_z = square(wave_z, 256)
        for j in range(3):
            square_yz = squares_y[j] + square_z
            for q in range(3):
                squared = square_yz + squares_x[q]
                logarithm = jnp.log(squared)
                place = (q, slice(tile * 8, tile * 8 + 8), slice(j * 128, j * 128 + 128))
                filters[(0, *place)] = jnp.exp(stiff_power * logarithm) * normalizer
                filters[(1, *place)] = (
                    jnp.exp(lossy_power * logarithm - filter_rate * squared) * normalizer
                )


def forward_x_kernel(device, pressure, tables, sent, filters, field, table, in_sems, table_sem):
    def load(h, g):
        return pltpu.make_async_copy(
            pressure.at[:, h, :, pl.ds(g * 128, 128)], field.at[h, g], in_sems.at[h, g]
        )

    load_table = pltpu.make_async_copy(tables.at[pl.ds(0, 4)], table, table_sem)
    for g in range(4):
        load(0, g).start()
    load_table.start()
    for g in range(4):
        load(1, g).start()
    write_filters(device[0], filters)
    load_table.wait()
    for h in range(2):
        for g in range(4):
            load(h, g).wait()
        views = [field.at[h, g].reshape(512, 128) for g in range(4)]
        blocks = [[], []]
        for group in range(2):
            near, far = [
                side(
                    [
                        jnp.concatenate(
                            [v[pl.ds(group * 4 + i, 64, stride=8), :] for i in range(4)], axis=0
                        )
                        for v in views[half * 2 : half * 2 + 2]
                    ]
                )
                for half in range(2)
            ]
            results = [
                even_forward(near + far, table),
                times_odd(near - far, table, True),
            ]
            for p in range(2):
                for i in range(4):
                    rows = results[p][i * 64 : i * 64 + 64]
                    block = jnp.concatenate([rows[:, :128], rows[:, 128:]], axis=0)
                    blocks[p].append(block.T)
        for p in range(2):
            sent[:, p, h] = jnp.swapaxes(jnp.stack(blocks[p], axis=0), 0, 1)


def plane_kernel(received, filters, tables, sent, spectrum, whole, filtered):
    chunks = [(high, x, core) for x in range(4) for high in range(2) for core in range(2)]
    for r in range(8):
        low, y = divmod(r, 4)
        plane = jnp.concatenate(
            [
                side([received[high, low, y, x, core, p] for p in range(2)])
                for high, x, core in chunks
            ],
            axis=0,
        )
        near, far = plane[:128], plane[128:]
        result = jnp.concatenate(
            [
                block_times(tables[SPLIT[0]], near + far),
                block_times(tables[SPLIT[1]], near - far),
            ],
            axis=0,
        )
        for p in range(2):
            spectrum[p, r] = result[:, p * 128 : p * 128 + 128]
    for p in range(2):
        columns = [[], []]
        for r in range(0, 8, 2):
            both = swap_halves(spectrum[p, r], spectrum[p, r + 1])
            for i in range(2):
                columns[i].append(both[i])
        for i in range(2):
            k = p * 2 + i
            near, far = side(columns[i][:2]), side(columns[i][2:])
            whole[k, :, :256] = even_forward(near + far, tables)
            whole[k, :, 256:] = times_odd(near - far, tables, True)
    for p in range(2):
        for f in range(2):
            backs = []
            for k in (p * 2, p * 2 + 1):
                q = min(k, 2)
                filter_rows = jnp.concatenate(
                    [
                        filters[f, q, 0:64],
                        filters[f, q, 128:136],
                        filters[f, q, 8:64],
                        filters[f, q, 64:128],
                        filters[f, q, 64:128],
                    ],
                    axis=0,
                )
                filter_odd = side([filter_rows[:, 256:], filter_rows[:, 256:]])
                back_even = even_back(whole[k, :, :256] * filter_rows[:, :256], tables)
                back_odd = times_odd(whole[k, :, 256:] * filter_odd, tables, False)
                backs.append(side([back_even + back_odd, back_even - back_odd]))
            for r in range(0, 8, 2):
                part = slice(r * 64, r * 64 + 128)
                both = swap_halves(backs[0][:, part], backs[1][:, part])
                for i in range(2):
                    filtered[f, r + i, p] = both[i]
    for r in range(8):
        low, y = divmod(r, 4)
        for f in range(2):
            even, odd = [
                block_times(
                    tables[SPLIT_BACK[i]],
                    side([filtered[f, r, p, i * 128 : i * 128 + 128] for p in range(2)]),
                )
                for i in range(2)
            ]
            field = jnp.concatenate([even + odd, even - odd], axis=0)
            for c, (high, x, core) in enumerate(chunks):
                for p in range(2):
                    sent[high, low, y, x, core, f, p] = field[
                        c * 16 : c * 16 + 16, p * 128 : p * 128 + 128
                    ]


def update_kernel(
    received,
    tables,
    pressure,
    pressure_prior,
    lossy_prior,
    stiffness,
    compensation,
    snapshot,
    image_prior,
    pressure_next,
    lossy_term,
    image_sum,
    terms,
    outputs,
    out_sems,
):
    sources = (
        pressure, pressure_prior, lossy_prior, stiffness, compensation, snapshot, image_prior
    )
    targets = (pressure_next, lossy_term, image_sum)

    def store(h, a, part):
        if a == 1:
            lanes = pl.ds(part * 128, 128)
            return pltpu.make_async_copy(
                terms.at[h, 1, part], targets[1].at[:, h, :, lanes], out_sems.at[h, 1, part]
            )
        mine = pl.ds((part - 1) * 16, 32)
        return pltpu.make_async_copy(
            outputs.at[h, a // 2, mine], targets[a].at[mine, h], out_sems.at[h, a, part]
        )

    def back_x(h, f):
        fields = [jnp.swapaxes(received[:, f, p, h], 0, 1) for p in range(2)]
        for group in range(2):
            rows = [[], []]
            for i in range(4):
                for p in range(2):
                    block = fields[p][group * 4 + i].T
                    rows[p].append(side([block[:64], block[64:]]))
            even = even_back(jnp.concatenate(rows[0], axis=0), tables)
            odd = times_odd(jnp.concatenate(rows[1], axis=0), tables, False)
            both = side([even + odd, even - odd])
            for g in range(4):
                view = terms.at[h, f, g].reshape(512, 128)
                for i in range(4):
                    view[pl.ds(group * 4 + i, 64, stride=8), :] = both[
                        i * 64 : i * 64 + 64, g * 128 : g * 128 + 128
                    ]

    for h in range(2):
        back_x(h, 1)
        for part in range(4):
            store(h, 1, part).start()
    for h in range(2):
        back_x(h, 0)
        for part in range(4):
            for y in range(part * 16, part * 16 + 16, 8):
                there = pl.ds(y, 8)
                stiff, lossy = [
                    jnp.concatenate([terms[h, f, g, there] for g in range(4)], axis=2)
                    for f in range(2)
                ]
                now, prior, loss, stiffs, comp, snap, image = [s[there, h] for s in sources]
                value = 2.0 * now - prior - stiffs * stiff + comp * (lossy - loss)
                outputs[h, 0, there] = value
                outputs[h, 1, there] = image + snap * value
            if part in PARTS:
                for a in (0, 2):
                    store(h, a, part).start()
    for h in range(2):
        for a in range(3):
            for part in (range(4) if a == 1 else PARTS):
                store(h, a, part).wait()


def held(array):
    return pltpu.with_memory_space_constraint(array, pltpu.VMEM)


def outer(array):
    return pltpu.with_memory_space_constraint(array, pltpu.HBM)


def call(kernel, operands, spaces, out_shape, scratch, limit):
    return pl.pallas_call(
        kernel,
        in_specs=[pl.BlockSpec(memory_space=space) for space in spaces],
        out_specs=[
            pl.BlockSpec(memory_space=pl.ANY if isinstance(s, jax.ShapeDtypeStruct) else pltpu.VMEM)
            for s in out_shape
        ],
        out_shape=out_shape,
        scratch_shapes=scratch,
        compiler_params=pltpu.CompilerParams(vmem_limit_bytes=limit * MIB),
    )(*operands)


def exchange(array, order):
    return lax.all_to_all(
        array, ("row", "col"), split_axis=0, concat_axis=0, tiled=True, axis_index_groups=[order]
    )


def body(pressure, pressure_prior, lossy_prior, stiffness, compensation, snapshot, image_prior):
    half, block = np.arange(256), np.arange(128)
    even_order = np.concatenate([block[:64], [64], block[:64:-1]])
    odd_order = np.concatenate([block[:64], block[:63:-1]])
    even_table = cas(even_order, block, 128)
    odd_table = cas(2 * odd_order + 1, block, 256)
    last_order = np.concatenate([half[:128], half[:127:-1]])
    tables = np.stack(
        [
            block_table(even_table),
            block_table(odd_table),
            *split_table(cas(2 * last_order + 1, half, 512)),
            block_table(even_table.T),
            block_table(odd_table.T),
        ]
    )
    place = np.arange(128).reshape(2, 4, 4, 2, 2)
    order = [int(i) for i in place.transpose(3, 0, 1, 2, 4).reshape(-1)]
    row, col = lax.axis_index("row"), lax.axis_index("col")
    device = (col // 2 % 2 * 2 + row // 4) * 32 + row % 4 * 8 + col // 4 * 2 + col % 2
    arrays = [
        a.reshape(64, 2, 8, 512)
        for a in (pressure, pressure_prior, lossy_prior, stiffness, compensation, snapshot, image_prior)
    ]
    f32 = jnp.float32
    dma = pltpu.SemaphoreType.DMA
    vmem = pltpu.VMEM

    sent, filters = call(
        forward_x_kernel,
        (device.reshape(1), outer(arrays[0]), outer(tables)),
        (pltpu.SMEM, pl.ANY, pl.ANY),
        [vmem((128, 2, 2, 8, 128), f32), vmem((2, 3, 136, 384), f32)],
        [
            vmem((2, 4, 64, 8, 128), f32),
            vmem((4, 256, 256), jnp.bfloat16),
            dma((2, 4)),
            dma,
        ],
        12,
    )
    received = exchange(sent.reshape(128, 32, 128), order)

    (sent,) = call(
        plane_kernel,
        (held(received.reshape(2, 2, 4, 4, 2, 2, 16, 128)), held(filters), held(tables)),
        (vmem, vmem, vmem),
        [vmem((2, 2, 4, 4, 2, 2, 2, 16, 128), f32)],
        [
            vmem((2, 8, 256, 128), f32),
            vmem((4, 256, 512), f32),
            vmem((2, 8, 2, 256, 128), f32),
        ],
        16,
    )
    received = exchange(sent.reshape(128, 64, 128), order)

    outs = call(
        update_kernel,
        (held(received.reshape(128, 2, 2, 2, 8, 128)), held(tables), *map(held, arrays)),
        (vmem,) * 9,
        [jax.ShapeDtypeStruct((64, 2, 8, 512), f32)] * 3,
        [
            vmem((2, 2, 4, 64, 8, 128), f32),
            vmem((2, 2, 64, 8, 512), f32),
            dma((2, 3, 4)),
        ],
        16,
    )
    return tuple(o.reshape(64, 16, 512) for o in outs)


def solution(mesh):
    spec = P("row", "col", None)
    return jax.shard_map(
        body, mesh=mesh, in_specs=(spec,) * 7, out_specs=(spec,) * 3, check_vma=False
    )
```

```python
import functools
import math

import jax
import jax.numpy as jnp
import ml_dtypes
import numpy as np
from jax import lax
from jax.experimental import pallas as pl
from jax.experimental.pallas import tpu as pltpu
from jax.sharding import PartitionSpec as P

stiff_power = 1.03
lossy_power = 0.53
filter_rate = 0.14
MIB = 1 << 20


def split_table(table):
    high = table.astype(ml_dtypes.bfloat16)
    low = (table - high.astype(np.float64)).astype(ml_dtypes.bfloat16)
    return high, low


def cas(left, right, length):
    angle = 2.0 * math.pi / length * (np.outer(left, right) % length)
    return np.cos(angle) + np.sin(angle)


def block_table(table):
    high, low = split_table(table)
    return np.block([[high, high], [low, low]])


def pieces(values):
    high = values.astype(jnp.bfloat16)
    low = (values - high.astype(jnp.float32)).astype(jnp.bfloat16)
    return high, low


SPLIT, ODD, SPLIT_BACK = (0, 1), 2, (4, 5)
PARTS = (1, 3)


def product(left, right, right_dim):
    return lax.dot_general(
        left, right, (((1,), (right_dim,)), ((), ())), preferred_element_type=jnp.float32
    )


def times_odd(values, tables, forward):
    axis = 1 if forward else 0
    left, table = list(pieces(values)), [tables[ODD], tables[ODD], tables[ODD + 1]]
    left.append(left[0])
    if forward:
        left.append(left[1])
        table.append(tables[ODD + 1])
    return product(jnp.concatenate(left, axis=1), jnp.concatenate(table, axis=axis), axis)


def times_block(values, table):
    both = product(jnp.concatenate(pieces(values), axis=1), table, 1)
    return both[:, :128] + both[:, 128:]


def block_times(table, values):
    both = product(table, jnp.concatenate(pieces(values), axis=0), 0)
    return both[:128] + both[128:]


def even_forward(values, tables):
    near, far = values[:, :128], values[:, 128:]
    return side([times_block(near + far, tables[SPLIT[0]]), times_block(near - far, tables[SPLIT[1]])])


def even_back(values, tables):
    even = times_block(values[:, :128], tables[SPLIT_BACK[0]])
    odd = times_block(values[:, 128:], tables[SPLIT_BACK[1]])
    return side([even + odd, even - odd])


def swap_halves(first, second):
    lane = lax.broadcasted_iota(jnp.int32, first.shape, 1)
    left = jnp.where(lane < 64, first, pltpu.roll(second, 64, 1))
    right = jnp.where(lane < 64, pltpu.roll(first, 64, 1), second)
    return left, right


def side(parts):
    return jnp.concatenate(parts, axis=1)


def write_filters(device, filters):
    normalizer = 1.0 / (512 * 256 * 512)
    lane = lax.broadcasted_iota(jnp.int32, (8, 128), 1)
    row = lax.broadcasted_iota(jnp.int32, (8, 128), 0)

    def waves(place):
        fourth = 4 * (place % 64)
        return [jnp.where(place == 64, 256, fourth), fourth + 2, 2 * place + 1]

    waves_y, waves_x = waves(lane), waves(device)

    def square(wave, length):
        return (2.0 * math.pi / length * wave.astype(jnp.float32)) ** 2

    squares_y = [square(wave, 512) for wave in waves_y]
    squares_x = [square(wave, 512) for wave in waves_x]
    for tile in range(17):
        wave_z = 2 * (row + tile % 8 * 8) + tile // 8 if tile < 16 else jnp.where(row == 0, 128, 2 * row)
        square_z = square(wave_z, 256)
        for j in range(3):
            square_yz = squares_y[j] + square_z
            for q in range(3):
                squared = square_yz + squares_x[q]
                logarithm = jnp.log(squared)
                place = (q, slice(tile * 8, tile * 8 + 8), slice(j * 128, j * 128 + 128))
                filters[(0, *place)] = jnp.exp(stiff_power * logarithm) * normalizer
                filters[(1, *place)] = (
                    jnp.exp(lossy_power * logarithm - filter_rate * squared) * normalizer
                )


def forward_x_kernel(device, pressure, tables, sent, filters, field, table, in_sems, table_sem):
    def load(h, g):
        return pltpu.make_async_copy(
            pressure.at[:, h, :, pl.ds(g * 128, 128)], field.at[h, g], in_sems.at[h, g]
        )

    load_table = pltpu.make_async_copy(tables.at[pl.ds(0, 4)], table, table_sem)
    for g in range(4):
        load(0, g).start()
    load_table.start()
    for g in range(4):
        load(1, g).start()
    write_filters(device[0], filters)
    load_table.wait()
    for h in range(2):
        for g in range(4):
            load(h, g).wait()
        views = [field.at[h, g].reshape(512, 128) for g in range(4)]
        blocks = [[], []]
        for group in range(2):
            near, far = [
                side(
                    [
                        jnp.concatenate(
                            [v[pl.ds(group * 4 + i, 64, stride=8), :] for i in range(4)], axis=0
                        )
                        for v in views[half * 2 : half * 2 + 2]
                    ]
                )
                for half in range(2)
            ]
            results = [
                even_forward(near + far, table),
                times_odd(near - far, table, True),
            ]
            for p in range(2):
                for i in range(4):
                    rows = results[p][i * 64 : i * 64 + 64]
                    block = jnp.concatenate([rows[:, :128], rows[:, 128:]], axis=0)
                    blocks[p].append(block.T)
        for p in range(2):
            sent[:, p, h] = jnp.swapaxes(jnp.stack(blocks[p], axis=0), 0, 1)


def plane_kernel(received, filters, tables, sent, spectrum, whole, filtered):
    chunks = [(high, x, core) for x in range(4) for high in range(2) for core in range(2)]
    for r in range(8):
        low, y = divmod(r, 4)
        plane = jnp.concatenate(
            [
                side([received[high, low, y, x, core, p] for p in range(2)])
                for high, x, core in chunks
            ],
            axis=0,
        )
        near, far = plane[:128], plane[128:]
        result = jnp.concatenate(
            [
                block_times(tables[SPLIT[0]], near + far),
                block_times(tables[SPLIT[1]], near - far),
            ],
            axis=0,
        )
        for p in range(2):
            spectrum[p, r] = result[:, p * 128 : p * 128 + 128]
    for p in range(2):
        columns = [[], []]
        for r in range(0, 8, 2):
            both = swap_halves(spectrum[p, r], spectrum[p, r + 1])
            for i in range(2):
                columns[i].append(both[i])
        for i in range(2):
            k = p * 2 + i
            near, far = side(columns[i][:2]), side(columns[i][2:])
            whole[k, :, :256] = even_forward(near + far, tables)
            whole[k, :, 256:] = times_odd(near - far, tables, True)
    for p in range(2):
        for f in range(2):
            backs = []
            for k in (p * 2, p * 2 + 1):
                q = min(k, 2)
                filter_rows = jnp.concatenate(
                    [
                        filters[f, q, 0:64],
                        filters[f, q, 128:136],
                        filters[f, q, 8:64],
                        filters[f, q, 64:128],
                        filters[f, q, 64:128],
                    ],
                    axis=0,
                )
                filter_odd = side([filter_rows[:, 256:], filter_rows[:, 256:]])
                back_even = even_back(whole[k, :, :256] * filter_rows[:, :256], tables)
                back_odd = times_odd(whole[k, :, 256:] * filter_odd, tables, False)
                backs.append(side([back_even + back_odd, back_even - back_odd]))
            for r in range(0, 8, 2):
                part = slice(r * 64, r * 64 + 128)
                both = swap_halves(backs[0][:, part], backs[1][:, part])
                for i in range(2):
                    filtered[f, r + i, p] = both[i]
    for r in range(8):
        low, y = divmod(r, 4)
        for f in range(2):
            even, odd = [
                block_times(
                    tables[SPLIT_BACK[i]],
                    side([filtered[f, r, p, i * 128 : i * 128 + 128] for p in range(2)]),
                )
                for i in range(2)
            ]
            field = jnp.concatenate([even + odd, even - odd], axis=0)
            for c, (high, x, core) in enumerate(chunks):
                for p in range(2):
                    sent[high, low, y, x, core, f, p] = field[
                        c * 16 : c * 16 + 16, p * 128 : p * 128 + 128
                    ]


def update_kernel(
    received,
    tables,
    pressure,
    pressure_prior,
    lossy_prior,
    stiffness,
    compensation,
    snapshot,
    image_prior,
    pressure_next,
    lossy_term,
    image_sum,
    terms,
    outputs,
    out_sems,
):
    sources = (
        pressure, pressure_prior, lossy_prior, stiffness, compensation, snapshot, image_prior
    )
    targets = (pressure_next, lossy_term, image_sum)

    def store(h, a, part):
        if a == 1:
            lanes = pl.ds(part * 128, 128)
            return pltpu.make_async_copy(
                terms.at[h, 1, part], targets[1].at[:, h, :, lanes], out_sems.at[h, 1, part]
            )
        mine = pl.ds((part - 1) * 16, 32)
        return pltpu.make_async_copy(
            outputs.at[h, a // 2, mine], targets[a].at[mine, h], out_sems.at[h, a, part]
        )

    def back_x(h, f):
        fields = [jnp.swapaxes(received[:, f, p, h], 0, 1) for p in range(2)]
        for group in range(2):
            rows = [[], []]
            for i in range(4):
                for p in range(2):
                    block = fields[p][group * 4 + i].T
                    rows[p].append(side([block[:64], block[64:]]))
            even = even_back(jnp.concatenate(rows[0], axis=0), tables)
            odd = times_odd(jnp.concatenate(rows[1], axis=0), tables, False)
            both = side([even + odd, even - odd])
            for g in range(4):
                view = terms.at[h, f, g].reshape(512, 128)
                for i in range(4):
                    view[pl.ds(group * 4 + i, 64, stride=8), :] = both[
                        i * 64 : i * 64 + 64, g * 128 : g * 128 + 128
                    ]

    for h in range(2):
        back_x(h, 1)
        for part in range(4):
            store(h, 1, part).start()
    for h in range(2):
        back_x(h, 0)
        for part in range(4):
            for y in range(part * 16, part * 16 + 16, 8):
                there = pl.ds(y, 8)
                stiff, lossy = [
                    jnp.concatenate([terms[h, f, g, there] for g in range(4)], axis=2)
                    for f in range(2)
                ]
                now, prior, loss, stiffs, comp, snap, image = [s[there, h] for s in sources]
                value = 2.0 * now - prior - stiffs * stiff + comp * (lossy - loss)
                outputs[h, 0, there] = value
                outputs[h, 1, there] = image + snap * value
            if part in PARTS:
                for a in (0, 2):
                    store(h, a, part).start()
    for h in range(2):
        for a in range(3):
            for part in (range(4) if a == 1 else PARTS):
                store(h, a, part).wait()


def held(array):
    return pltpu.with_memory_space_constraint(array, pltpu.VMEM)


def outer(array):
    return pltpu.with_memory_space_constraint(array, pltpu.HBM)


def call(kernel, operands, spaces, out_shape, scratch, limit):
    return pl.pallas_call(
        kernel,
        in_specs=[pl.BlockSpec(memory_space=space) for space in spaces],
        out_specs=[
            pl.BlockSpec(memory_space=pl.ANY if isinstance(s, jax.ShapeDtypeStruct) else pltpu.VMEM)
            for s in out_shape
        ],
        out_shape=out_shape,
        scratch_shapes=scratch,
        compiler_params=pltpu.CompilerParams(vmem_limit_bytes=limit * MIB),
    )(*operands)


def exchange(array, order):
    return lax.all_to_all(
        array, ("row", "col"), split_axis=0, concat_axis=0, tiled=True, axis_index_groups=[order]
    )


def body(pressure, pressure_prior, lossy_prior, stiffness, compensation, snapshot, image_prior):
    half, block = np.arange(256), np.arange(128)
    even_order = np.concatenate([block[:64], [64], block[:64:-1]])
    odd_order = np.concatenate([block[:64], block[:63:-1]])
    even_table = cas(even_order, block, 128)
    odd_table = cas(2 * odd_order + 1, block, 256)
    last_order = np.concatenate([half[:128], half[:127:-1]])
    tables = np.stack(
        [
            block_table(even_table),
            block_table(odd_table),
            *split_table(cas(2 * last_order + 1, half, 512)),
            block_table(even_table.T),
            block_table(odd_table.T),
        ]
    )
    place = np.arange(128).reshape(2, 4, 4, 2, 2)
    order = [int(i) for i in place.transpose(3, 0, 1, 2, 4).reshape(-1)]
    row, col = lax.axis_index("row"), lax.axis_index("col")
    device = (col // 2 % 2 * 2 + row // 4) * 32 + row % 4 * 8 + col // 4 * 2 + col % 2
    arrays = [
        a.reshape(64, 2, 8, 512)
        for a in (pressure, pressure_prior, lossy_prior, stiffness, compensation, snapshot, image_prior)
    ]
    f32 = jnp.float32
    dma = pltpu.SemaphoreType.DMA
    vmem = pltpu.VMEM

    sent, filters = call(
        forward_x_kernel,
        (device.reshape(1), outer(arrays[0]), outer(tables)),
        (pltpu.SMEM, pl.ANY, pl.ANY),
        [vmem((128, 2, 2, 8, 128), f32), vmem((2, 3, 136, 384), f32)],
        [
            vmem((2, 4, 64, 8, 128), f32),
            vmem((4, 256, 256), jnp.bfloat16),
            dma((2, 4)),
            dma,
        ],
        12,
    )
    received = exchange(sent.reshape(128, 32, 128), order)

    (sent,) = call(
        plane_kernel,
        (held(received.reshape(2, 2, 4, 4, 2, 2, 16, 128)), held(filters), held(tables)),
        (vmem, vmem, vmem),
        [vmem((2, 2, 4, 4, 2, 2, 2, 16, 128), f32)],
        [
            vmem((2, 8, 256, 128), f32),
            vmem((4, 256, 512), f32),
            vmem((2, 8, 2, 256, 128), f32),
        ],
        16,
    )
    received = exchange(sent.reshape(128, 64, 128), order)

    outs = call(
        update_kernel,
        (held(received.reshape(128, 2, 2, 2, 8, 128)), held(tables), *map(held, arrays)),
        (vmem,) * 9,
        [jax.ShapeDtypeStruct((64, 2, 8, 512), f32)] * 3,
        [
            vmem((2, 2, 4, 64, 8, 128), f32),
            vmem((2, 2, 64, 8, 512), f32),
            dma((2, 3, 4)),
        ],
        16,
    )
    return tuple(o.reshape(64, 16, 512) for o in outs)


def solution(mesh):
    spec = P("row", "col", None)
    return jax.shard_map(
        body, mesh=mesh, in_specs=(spec,) * 7, out_specs=(spec,) * 3, check_vma=False
    )
```

```python
import functools
import math

import jax
import jax.numpy as jnp
import ml_dtypes
import numpy as np
from jax import lax
from jax.experimental import pallas as pl
from jax.experimental.pallas import tpu as pltpu
from jax.sharding import PartitionSpec as P

stiff_power = 1.03
lossy_power = 0.53
filter_rate = 0.14
MIB = 1 << 20


def split_table(table):
    high = table.astype(ml_dtypes.bfloat16)
    low = (table - high.astype(np.float64)).astype(ml_dtypes.bfloat16)
    return high, low


def cas(left, right, length):
    angle = 2.0 * math.pi / length * (np.outer(left, right) % length)
    return np.cos(angle) + np.sin(angle)


def block_table(table):
    high, low = split_table(table)
    return np.block([[high, high], [low, low]])


def rest_table(table):
    high, low = split_table(table)
    rest = (table - high.astype(np.float64) - low.astype(np.float64)).astype(ml_dtypes.bfloat16)
    return np.block([[high, rest], [np.zeros_like(high), np.zeros_like(high)]])


def pieces(values):
    high = values.astype(jnp.bfloat16)
    low = (values - high.astype(jnp.float32)).astype(jnp.bfloat16)
    return high, low


SPLIT, ODD, SPLIT_REST, SPLIT_BACK = (0, 1), 2, (5, 6), (7, 8)
PARTS = (1, 3)


def product(left, right, right_dim):
    return lax.dot_general(
        left, right, (((1,), (right_dim,)), ((), ())), preferred_element_type=jnp.float32
    )


def three_pieces(values):
    high, low = pieces(values)
    rest = values - high.astype(jnp.float32) - low.astype(jnp.float32)
    return high, low, rest.astype(jnp.bfloat16)


def odd_forward(values, tables):
    high, low, rest = three_pieces(values)
    first, second, third = [tables[ODD + i] for i in range(3)]
    left = side([high, low, high, low, rest, high])
    return product(left, side([first, first, second, second, first, third]), 1)


def odd_back(values, tables):
    high, low = pieces(values)
    table = jnp.concatenate([tables[ODD], tables[ODD], tables[ODD + 1]], axis=0)
    return product(side([high, low, high]), table, 0)


def forward_table(tables, i):
    return side([tables[SPLIT[i]], tables[SPLIT_REST[i]]])


def times_block(values, table, forward):
    if forward:
        high, low, rest = three_pieces(values)
        left = side([high, low, rest, high])
    else:
        left = side(pieces(values))
    both = product(left, table, 1)
    return both[:, :128] + both[:, 128:]


def block_times(table, values, rest_table=None):
    if rest_table is None:
        both = product(table, jnp.concatenate(pieces(values), axis=0), 0)
        return both[:128] + both[128:]
    high, low, rest = three_pieces(values)
    both = product(table, jnp.concatenate([high, low], axis=0), 0)
    third = product(rest_table[:128], jnp.concatenate([rest, high], axis=0), 0)
    return both[:128] + (both[128:] + third)


def even_forward(values, tables):
    near, far = values[:, :128], values[:, 128:]
    return side(
        [
            times_block(near + far, forward_table(tables, 0), True),
            times_block(near - far, forward_table(tables, 1), True),
        ]
    )


def even_back(values, tables):
    even = times_block(values[:, :128], tables[SPLIT_BACK[0]], False)
    odd = times_block(values[:, 128:], tables[SPLIT_BACK[1]], False)
    return side([even + odd, even - odd])


def swap_halves(first, second):
    lane = lax.broadcasted_iota(jnp.int32, first.shape, 1)
    left = jnp.where(lane < 64, first, pltpu.roll(second, 64, 1))
    right = jnp.where(lane < 64, pltpu.roll(first, 64, 1), second)
    return left, right


def side(parts):
    return jnp.concatenate(parts, axis=1)


def write_filters(device, filters):
    normalizer = 1.0 / (512 * 256 * 512)
    lane = lax.broadcasted_iota(jnp.int32, (8, 128), 1)
    row = lax.broadcasted_iota(jnp.int32, (8, 128), 0)

    def waves(place):
        fourth = 4 * (place % 64)
        return [jnp.where(place == 64, 256, fourth), fourth + 2, 2 * place + 1]

    waves_y, waves_x = waves(lane), waves(device)

    def square(wave, length):
        return (2.0 * math.pi / length * wave.astype(jnp.float32)) ** 2

    squares_y = [square(wave, 512) for wave in waves_y]
    squares_x = [square(wave, 512) for wave in waves_x]
    for tile in range(17):
        wave_z = 2 * (row + tile % 8 * 8) + tile // 8 if tile < 16 else jnp.where(row == 0, 128, 2 * row)
        square_z = square(wave_z, 256)
        for j in range(3):
            square_yz = squares_y[j] + square_z
            for q in range(3):
                squared = square_yz + squares_x[q]
                logarithm = jnp.log(squared)
                place = (q, slice(tile * 8, tile * 8 + 8), slice(j * 128, j * 128 + 128))
                filters[(0, *place)] = jnp.exp(stiff_power * logarithm) * normalizer
                filters[(1, *place)] = (
                    jnp.exp(lossy_power * logarithm - filter_rate * squared) * normalizer
                )


def forward_x_kernel(device, pressure, tables, sent, filters, field, table, in_sems, table_sem):
    def load(h, g):
        return pltpu.make_async_copy(
            pressure.at[:, h, :, pl.ds(g * 128, 128)], field.at[h, g], in_sems.at[h, g]
        )

    load_table = pltpu.make_async_copy(tables.at[pl.ds(0, 7)], table, table_sem)
    for g in range(4):
        load(0, g).start()
    load_table.start()
    for g in range(4):
        load(1, g).start()
    write_filters(device[0], filters)
    load_table.wait()
    for h in range(2):
        for g in range(4):
            load(h, g).wait()
        views = [field.at[h, g].reshape(512, 128) for g in range(4)]
        blocks = [[], []]
        for group in range(2):
            near, far = [
                side(
                    [
                        jnp.concatenate(
                            [v[pl.ds(group * 4 + i, 64, stride=8), :] for i in range(4)], axis=0
                        )
                        for v in views[half * 2 : half * 2 + 2]
                    ]
                )
                for half in range(2)
            ]
            results = [
                even_forward(near + far, table),
                odd_forward(near - far, table),
            ]
            for p in range(2):
                for i in range(4):
                    rows = results[p][i * 64 : i * 64 + 64]
                    block = jnp.concatenate([rows[:, :128], rows[:, 128:]], axis=0)
                    blocks[p].append(block.T)
        for p in range(2):
            sent[:, p, h] = jnp.swapaxes(jnp.stack(blocks[p], axis=0), 0, 1)


def plane_kernel(received, filters, tables, sent, spectrum, whole, filtered):
    chunks = [(high, x, core) for x in range(4) for high in range(2) for core in range(2)]
    for r in range(8):
        low, y = divmod(r, 4)
        plane = jnp.concatenate(
            [
                side([received[high, low, y, x, core, p] for p in range(2)])
                for high, x, core in chunks
            ],
            axis=0,
        )
        near, far = plane[:128], plane[128:]
        result = jnp.concatenate(
            [
                block_times(tables[SPLIT[0]], near + far, tables[SPLIT_REST[0]]),
                block_times(tables[SPLIT[1]], near - far, tables[SPLIT_REST[1]]),
            ],
            axis=0,
        )
        for p in range(2):
            spectrum[p, r] = result[:, p * 128 : p * 128 + 128]
    for p in range(2):
        columns = [[], []]
        for r in range(0, 8, 2):
            both = swap_halves(spectrum[p, r], spectrum[p, r + 1])
            for i in range(2):
                columns[i].append(both[i])
        for i in range(2):
            k = p * 2 + i
            near, far = side(columns[i][:2]), side(columns[i][2:])
            whole[k, :, :256] = even_forward(near + far, tables)
            whole[k, :, 256:] = odd_forward(near - far, tables)
    for p in range(2):
        for f in range(2):
            backs = []
            for k in (p * 2, p * 2 + 1):
                q = min(k, 2)
                filter_rows = jnp.concatenate(
                    [
                        filters[f, q, 0:64],
                        filters[f, q, 128:136],
                        filters[f, q, 8:64],
                        filters[f, q, 64:128],
                        filters[f, q, 64:128],
                    ],
                    axis=0,
                )
                filter_odd = side([filter_rows[:, 256:], filter_rows[:, 256:]])
                back_even = even_back(whole[k, :, :256] * filter_rows[:, :256], tables)
                back_odd = odd_back(whole[k, :, 256:] * filter_odd, tables)
                backs.append(side([back_even + back_odd, back_even - back_odd]))
            for r in range(0, 8, 2):
                part = slice(r * 64, r * 64 + 128)
                both = swap_halves(backs[0][:, part], backs[1][:, part])
                for i in range(2):
                    filtered[f, r + i, p] = both[i]
    for r in range(8):
        low, y = divmod(r, 4)
        for f in range(2):
            even, odd = [
                block_times(
                    tables[SPLIT_BACK[i]],
                    side([filtered[f, r, p, i * 128 : i * 128 + 128] for p in range(2)]),
                )
                for i in range(2)
            ]
            field = jnp.concatenate([even + odd, even - odd], axis=0)
            for c, (high, x, core) in enumerate(chunks):
                for p in range(2):
                    sent[high, low, y, x, core, f, p] = field[
                        c * 16 : c * 16 + 16, p * 128 : p * 128 + 128
                    ]


def update_kernel(
    received,
    tables,
    pressure,
    pressure_prior,
    lossy_prior,
    stiffness,
    compensation,
    snapshot,
    image_prior,
    pressure_next,
    lossy_term,
    image_sum,
    terms,
    outputs,
    out_sems,
):
    sources = (
        pressure, pressure_prior, lossy_prior, stiffness, compensation, snapshot, image_prior
    )
    targets = (pressure_next, lossy_term, image_sum)

    def store(h, a, part):
        if a == 1:
            lanes = pl.ds(part * 128, 128)
            return pltpu.make_async_copy(
                terms.at[h, 1, part], targets[1].at[:, h, :, lanes], out_sems.at[h, 1, part]
            )
        mine = pl.ds((part - 1) * 16, 32)
        return pltpu.make_async_copy(
            outputs.at[h, a // 2, mine], targets[a].at[mine, h], out_sems.at[h, a, part]
        )

    def back_x(h, f):
        fields = [jnp.swapaxes(received[:, f, p, h], 0, 1) for p in range(2)]
        for group in range(2):
            rows = [[], []]
            for i in range(4):
                for p in range(2):
                    block = fields[p][group * 4 + i].T
                    rows[p].append(side([block[:64], block[64:]]))
            even = even_back(jnp.concatenate(rows[0], axis=0), tables)
            odd = odd_back(jnp.concatenate(rows[1], axis=0), tables)
            both = side([even + odd, even - odd])
            for g in range(4):
                view = terms.at[h, f, g].reshape(512, 128)
                for i in range(4):
                    view[pl.ds(group * 4 + i, 64, stride=8), :] = both[
                        i * 64 : i * 64 + 64, g * 128 : g * 128 + 128
                    ]

    for h in range(2):
        back_x(h, 1)
        for part in range(4):
            store(h, 1, part).start()
    for h in range(2):
        back_x(h, 0)
        for part in range(4):
            for y in range(part * 16, part * 16 + 16, 8):
                there = pl.ds(y, 8)
                stiff, lossy = [
                    jnp.concatenate([terms[h, f, g, there] for g in range(4)], axis=2)
                    for f in range(2)
                ]
                now, prior, loss, stiffs, comp, snap, image = [s[there, h] for s in sources]
                value = 2.0 * now - prior - stiffs * stiff + comp * (lossy - loss)
                outputs[h, 0, there] = value
                outputs[h, 1, there] = image + snap * value
            if part in PARTS:
                for a in (0, 2):
                    store(h, a, part).start()
    for h in range(2):
        for a in range(3):
            for part in (range(4) if a == 1 else PARTS):
                store(h, a, part).wait()


def held(array):
    return pltpu.with_memory_space_constraint(array, pltpu.VMEM)


def outer(array):
    return pltpu.with_memory_space_constraint(array, pltpu.HBM)


def call(kernel, operands, spaces, out_shape, scratch, limit):
    return pl.pallas_call(
        kernel,
        in_specs=[pl.BlockSpec(memory_space=space) for space in spaces],
        out_specs=[
            pl.BlockSpec(memory_space=pl.ANY if isinstance(s, jax.ShapeDtypeStruct) else pltpu.VMEM)
            for s in out_shape
        ],
        out_shape=out_shape,
        scratch_shapes=scratch,
        compiler_params=pltpu.CompilerParams(vmem_limit_bytes=limit * MIB),
    )(*operands)


def exchange(array, order):
    return lax.all_to_all(
        array, ("row", "col"), split_axis=0, concat_axis=0, tiled=True, axis_index_groups=[order]
    )


def body(pressure, pressure_prior, lossy_prior, stiffness, compensation, snapshot, image_prior):
    half, block = np.arange(256), np.arange(128)
    even_order = np.concatenate([block[:64], [64], block[:64:-1]])
    odd_order = np.concatenate([block[:64], block[:63:-1]])
    even_table = cas(even_order, block, 128)
    odd_table = cas(2 * odd_order + 1, block, 256)
    last_order = np.concatenate([half[:128], half[:127:-1]])
    last_table = cas(2 * last_order + 1, half, 512)
    tables = np.stack(
        [
            block_table(even_table),
            block_table(odd_table),
            *split_table(last_table),
            rest_table(last_table)[:256, 256:],
            rest_table(even_table),
            rest_table(odd_table),
            block_table(even_table.T),
            block_table(odd_table.T),
        ]
    )
    place = np.arange(128).reshape(2, 4, 4, 2, 2)
    order = [int(i) for i in place.transpose(3, 0, 1, 2, 4).reshape(-1)]
    row, col = lax.axis_index("row"), lax.axis_index("col")
    device = (col // 2 % 2 * 2 + row // 4) * 32 + row % 4 * 8 + col // 4 * 2 + col % 2
    arrays = [
        a.reshape(64, 2, 8, 512)
        for a in (pressure, pressure_prior, lossy_prior, stiffness, compensation, snapshot, image_prior)
    ]
    f32 = jnp.float32
    dma = pltpu.SemaphoreType.DMA
    vmem = pltpu.VMEM

    sent, filters = call(
        forward_x_kernel,
        (device.reshape(1), outer(arrays[0]), outer(tables)),
        (pltpu.SMEM, pl.ANY, pl.ANY),
        [vmem((128, 2, 2, 8, 128), f32), vmem((2, 3, 136, 384), f32)],
        [
            vmem((2, 4, 64, 8, 128), f32),
            vmem((7, 256, 256), jnp.bfloat16),
            dma((2, 4)),
            dma,
        ],
        12,
    )
    received = exchange(sent.reshape(128, 32, 128), order)

    (sent,) = call(
        plane_kernel,
        (held(received.reshape(2, 2, 4, 4, 2, 2, 16, 128)), held(filters), held(tables)),
        (vmem, vmem, vmem),
        [vmem((2, 2, 4, 4, 2, 2, 2, 16, 128), f32)],
        [
            vmem((2, 8, 256, 128), f32),
            vmem((4, 256, 512), f32),
            vmem((2, 8, 2, 256, 128), f32),
        ],
        16,
    )
    received = exchange(sent.reshape(128, 64, 128), order)

    outs = call(
        update_kernel,
        (held(received.reshape(128, 2, 2, 2, 8, 128)), held(tables), *map(held, arrays)),
        (vmem,) * 9,
        [jax.ShapeDtypeStruct((64, 2, 8, 512), f32)] * 3,
        [
            vmem((2, 2, 4, 64, 8, 128), f32),
            vmem((2, 2, 64, 8, 512), f32),
            dma((2, 3, 4)),
        ],
        16,
    )
    return tuple(o.reshape(64, 16, 512) for o in outs)


def solution(mesh):
    spec = P("row", "col", None)
    return jax.shard_map(
        body, mesh=mesh, in_specs=(spec,) * 7, out_specs=(spec,) * 3, check_vma=False
    )
```

```python
import functools
import math

import jax
import jax.numpy as jnp
import ml_dtypes
import numpy as np
from jax import lax
from jax.experimental import pallas as pl
from jax.experimental.pallas import tpu as pltpu
from jax.sharding import PartitionSpec as P

stiff_power = 1.03
lossy_power = 0.53
filter_rate = 0.14
MIB = 1 << 20


def split_table(table):
    high = table.astype(ml_dtypes.bfloat16)
    low = (table - high.astype(np.float64)).astype(ml_dtypes.bfloat16)
    return high, low


def cas(left, right, length):
    angle = 2.0 * math.pi / length * (np.outer(left, right) % length)
    return np.cos(angle) + np.sin(angle)


def block_table(table):
    high, low = split_table(table)
    return np.block([[high, high], [low, low]])


def rest_table(table):
    high, low = split_table(table)
    rest = (table - high.astype(np.float64) - low.astype(np.float64)).astype(ml_dtypes.bfloat16)
    return np.block([[high, rest], [np.zeros_like(high), np.zeros_like(high)]])


def pieces(values):
    high = values.astype(jnp.bfloat16)
    low = (values - high.astype(jnp.float32)).astype(jnp.bfloat16)
    return high, low


SPLIT, ODD, SPLIT_REST, SPLIT_BACK = (0, 1), 2, (5, 6), (7, 8)
PARTS = (1, 3)


def product(left, right, right_dim):
    return lax.dot_general(
        left, right, (((1,), (right_dim,)), ((), ())), preferred_element_type=jnp.float32
    )


def three_pieces(values):
    high, low = pieces(values)
    rest = values - high.astype(jnp.float32) - low.astype(jnp.float32)
    return high, low, rest.astype(jnp.bfloat16)


def odd_forward(values, tables):
    high, low, rest = three_pieces(values)
    first, second, third = [tables[ODD + i] for i in range(3)]
    left = side([high, low, high, low, rest, high])
    return product(left, side([first, first, second, second, first, third]), 1)


def odd_back(values, tables):
    high, low = pieces(values)
    table = jnp.concatenate([tables[ODD], tables[ODD], tables[ODD + 1]], axis=0)
    return product(side([high, low, high]), table, 0)


def forward_table(tables, i):
    return side([tables[SPLIT[i]], tables[SPLIT_REST[i]]])


def times_block(values, table, forward):
    if forward:
        high, low, rest = three_pieces(values)
        left = side([high, low, rest, high])
    else:
        left = side(pieces(values))
    both = product(left, table, 1)
    return both[:, :128] + both[:, 128:]


def block_times(table, values, rest_table=None):
    if rest_table is None:
        both = product(table, jnp.concatenate(pieces(values), axis=0), 0)
        return both[:128] + both[128:]
    high, low, rest = three_pieces(values)
    both = product(table, jnp.concatenate([high, low], axis=0), 0)
    third = product(rest_table[:128], jnp.concatenate([rest, high], axis=0), 0)
    return both[:128] + (both[128:] + third)


def even_forward(values, tables):
    near, far = values[:, :128], values[:, 128:]
    return side(
        [
            times_block(near + far, forward_table(tables, 0), True),
            times_block(near - far, forward_table(tables, 1), True),
        ]
    )


def even_back(values, tables):
    even = times_block(values[:, :128], tables[SPLIT_BACK[0]], False)
    odd = times_block(values[:, 128:], tables[SPLIT_BACK[1]], False)
    return side([even + odd, even - odd])


def swap_halves(first, second):
    lane = lax.broadcasted_iota(jnp.int32, first.shape, 1)
    left = jnp.where(lane < 64, first, pltpu.roll(second, 64, 1))
    right = jnp.where(lane < 64, pltpu.roll(first, 64, 1), second)
    return left, right


def side(parts):
    return jnp.concatenate(parts, axis=1)


def write_filters(device, filters):
    normalizer = 1.0 / (512 * 256 * 512)
    lane = lax.broadcasted_iota(jnp.int32, (8, 128), 1)
    row = lax.broadcasted_iota(jnp.int32, (8, 128), 0)

    def waves(place):
        fourth = 4 * (place % 64)
        return [jnp.where(place == 64, 256, fourth), fourth + 2, 2 * place + 1]

    waves_y, waves_x = waves(lane), waves(device)

    def square(wave, length):
        return (2.0 * math.pi / length * wave.astype(jnp.float32)) ** 2

    squares_y = [square(wave, 512) for wave in waves_y]
    squares_x = [square(wave, 512) for wave in waves_x]
    for tile in range(17):
        wave_z = 2 * (row + tile % 8 * 8) + tile // 8 if tile < 16 else jnp.where(row == 0, 128, 2 * row)
        square_z = square(wave_z, 256)
        for j in range(3):
            square_yz = squares_y[j] + square_z
            for q in range(3):
                squared = square_yz + squares_x[q]
                logarithm = jnp.log(squared)
                place = (q, slice(tile * 8, tile * 8 + 8), slice(j * 128, j * 128 + 128))
                filters[(0, *place)] = jnp.exp(stiff_power * logarithm) * normalizer
                filters[(1, *place)] = (
                    jnp.exp(lossy_power * logarithm - filter_rate * squared) * normalizer
                )


def forward_x_kernel(device, pressure, tables, sent, filters, field, table, in_sems, table_sem):
    def load(h, g):
        return pltpu.make_async_copy(
            pressure.at[:, h, :, pl.ds(g * 128, 128)], field.at[h, g], in_sems.at[h, g]
        )

    load_table = pltpu.make_async_copy(tables.at[pl.ds(0, 7)], table, table_sem)
    for g in range(4):
        load(0, g).start()
    load_table.start()
    for g in range(4):
        load(1, g).start()
    write_filters(device[0], filters)
    load_table.wait()
    for h in range(2):
        for g in range(4):
            load(h, g).wait()
        views = [field.at[h, g].reshape(512, 128) for g in range(4)]
        blocks = [[], []]
        for group in range(2):
            near, far = [
                side(
                    [
                        jnp.concatenate(
                            [v[pl.ds(group * 4 + i, 64, stride=8), :] for i in range(4)], axis=0
                        )
                        for v in views[half * 2 : half * 2 + 2]
                    ]
                )
                for half in range(2)
            ]
            results = [
                even_forward(near + far, table),
                odd_forward(near - far, table),
            ]
            for p in range(2):
                for i in range(4):
                    rows = results[p][i * 64 : i * 64 + 64]
                    block = jnp.concatenate([rows[:, :128], rows[:, 128:]], axis=0)
                    blocks[p].append(block.T)
        for p in range(2):
            sent[:, p, h] = jnp.swapaxes(jnp.stack(blocks[p], axis=0), 0, 1)


def plane_kernel(received, filters, tables, sent, spectrum, whole, filtered):
    chunks = [(high, x, core) for x in range(4) for high in range(2) for core in range(2)]
    for r in range(8):
        low, y = divmod(r, 4)
        plane = jnp.concatenate(
            [
                side([received[high, low, y, x, core, p] for p in range(2)])
                for high, x, core in chunks
            ],
            axis=0,
        )
        near, far = plane[:128], plane[128:]
        result = jnp.concatenate(
            [
                block_times(tables[SPLIT[0]], near + far, tables[SPLIT_REST[0]]),
                block_times(tables[SPLIT[1]], near - far, tables[SPLIT_REST[1]]),
            ],
            axis=0,
        )
        for p in range(2):
            spectrum[p, r] = result[:, p * 128 : p * 128 + 128]
    for p in range(2):
        columns = [[], []]
        for r in range(0, 8, 2):
            both = swap_halves(spectrum[p, r], spectrum[p, r + 1])
            for i in range(2):
                columns[i].append(both[i])
        for i in range(2):
            k = p * 2 + i
            near, far = side(columns[i][:2]), side(columns[i][2:])
            whole[k, :, :256] = even_forward(near + far, tables)
            whole[k, :, 256:] = odd_forward(near - far, tables)
    for p in range(2):
        for f in range(2):
            backs = []
            for k in (p * 2, p * 2 + 1):
                q = min(k, 2)
                filter_rows = jnp.concatenate(
                    [
                        filters[f, q, 0:64],
                        filters[f, q, 128:136],
                        filters[f, q, 8:64],
                        filters[f, q, 64:128],
                        filters[f, q, 64:128],
                    ],
                    axis=0,
                )
                filter_odd = side([filter_rows[:, 256:], filter_rows[:, 256:]])
                back_even = even_back(whole[k, :, :256] * filter_rows[:, :256], tables)
                back_odd = odd_back(whole[k, :, 256:] * filter_odd, tables)
                backs.append(side([back_even + back_odd, back_even - back_odd]))
            for r in range(0, 8, 2):
                part = slice(r * 64, r * 64 + 128)
                both = swap_halves(backs[0][:, part], backs[1][:, part])
                for i in range(2):
                    filtered[f, r + i, p] = both[i]
    for r in range(8):
        low, y = divmod(r, 4)
        for f in range(2):
            even, odd = [
                block_times(
                    tables[SPLIT_BACK[i]],
                    side([filtered[f, r, p, i * 128 : i * 128 + 128] for p in range(2)]),
                )
                for i in range(2)
            ]
            field = jnp.concatenate([even + odd, even - odd], axis=0)
            for c, (high, x, core) in enumerate(chunks):
                for p in range(2):
                    sent[high, low, y, x, core, f, p] = field[
                        c * 16 : c * 16 + 16, p * 128 : p * 128 + 128
                    ]


def update_kernel(
    received,
    tables,
    pressure,
    pressure_prior,
    lossy_prior,
    stiffness,
    compensation,
    snapshot,
    image_prior,
    pressure_next,
    lossy_term,
    image_sum,
    terms,
    outputs,
    out_sems,
):
    sources = (
        pressure, pressure_prior, lossy_prior, stiffness, compensation, snapshot, image_prior
    )
    targets = (pressure_next, lossy_term, image_sum)

    def store(h, a, part):
        if a == 1:
            lanes = pl.ds(part * 128, 128)
            return pltpu.make_async_copy(
                terms.at[h, 1, part], targets[1].at[:, h, :, lanes], out_sems.at[h, 1, part]
            )
        mine = pl.ds((part - 1) * 16, 32)
        return pltpu.make_async_copy(
            outputs.at[h, a // 2, mine], targets[a].at[mine, h], out_sems.at[h, a, part]
        )

    def back_x(h, f):
        fields = [jnp.swapaxes(received[:, f, p, h], 0, 1) for p in range(2)]
        for group in range(2):
            rows = [[], []]
            for i in range(4):
                for p in range(2):
                    block = fields[p][group * 4 + i].T
                    rows[p].append(side([block[:64], block[64:]]))
            even = even_back(jnp.concatenate(rows[0], axis=0), tables)
            odd = odd_back(jnp.concatenate(rows[1], axis=0), tables)
            both = side([even + odd, even - odd])
            for g in range(4):
                view = terms.at[h, f, g].reshape(512, 128)
                for i in range(4):
                    view[pl.ds(group * 4 + i, 64, stride=8), :] = both[
                        i * 64 : i * 64 + 64, g * 128 : g * 128 + 128
                    ]

    for h in range(2):
        back_x(h, 1)
    for h in range(2):
        for part in range(4):
            store(h, 1, part).start()
    for h in range(2):
        back_x(h, 0)
        for part in range(4):
            for y in range(part * 16, part * 16 + 16, 8):
                there = pl.ds(y, 8)
                stiff, lossy = [
                    jnp.concatenate([terms[h, f, g, there] for g in range(4)], axis=2)
                    for f in range(2)
                ]
                now, prior, loss, stiffs, comp, snap, image = [s[there, h] for s in sources]
                value = 2.0 * now - prior - stiffs * stiff + comp * (lossy - loss)
                outputs[h, 0, there] = value
                outputs[h, 1, there] = image + snap * value
            if part in PARTS:
                for a in (0, 2):
                    store(h, a, part).start()
    for h in range(2):
        for a in range(3):
            for part in (range(4) if a == 1 else PARTS):
                store(h, a, part).wait()


def held(array):
    return pltpu.with_memory_space_constraint(array, pltpu.VMEM)


def outer(array):
    return pltpu.with_memory_space_constraint(array, pltpu.HBM)


def call(kernel, operands, spaces, out_shape, scratch, limit):
    return pl.pallas_call(
        kernel,
        in_specs=[pl.BlockSpec(memory_space=space) for space in spaces],
        out_specs=[
            pl.BlockSpec(memory_space=pl.ANY if isinstance(s, jax.ShapeDtypeStruct) else pltpu.VMEM)
            for s in out_shape
        ],
        out_shape=out_shape,
        scratch_shapes=scratch,
        compiler_params=pltpu.CompilerParams(vmem_limit_bytes=limit * MIB),
    )(*operands)


def exchange(array, order):
    return lax.all_to_all(
        array, ("row", "col"), split_axis=0, concat_axis=0, tiled=True, axis_index_groups=[order]
    )


def body(pressure, pressure_prior, lossy_prior, stiffness, compensation, snapshot, image_prior):
    half, block = np.arange(256), np.arange(128)
    even_order = np.concatenate([block[:64], [64], block[:64:-1]])
    odd_order = np.concatenate([block[:64], block[:63:-1]])
    even_table = cas(even_order, block, 128)
    odd_table = cas(2 * odd_order + 1, block, 256)
    last_order = np.concatenate([half[:128], half[:127:-1]])
    last_table = cas(2 * last_order + 1, half, 512)
    tables = np.stack(
        [
            block_table(even_table),
            block_table(odd_table),
            *split_table(last_table),
            rest_table(last_table)[:256, 256:],
            rest_table(even_table),
            rest_table(odd_table),
            block_table(even_table.T),
            block_table(odd_table.T),
        ]
    )
    place = np.arange(128).reshape(2, 4, 4, 2, 2)
    order = [int(i) for i in place.transpose(3, 0, 1, 2, 4).reshape(-1)]
    row, col = lax.axis_index("row"), lax.axis_index("col")
    device = (col // 2 % 2 * 2 + row // 4) * 32 + row % 4 * 8 + col // 4 * 2 + col % 2
    arrays = [
        a.reshape(64, 2, 8, 512)
        for a in (pressure, pressure_prior, lossy_prior, stiffness, compensation, snapshot, image_prior)
    ]
    f32 = jnp.float32
    dma = pltpu.SemaphoreType.DMA
    vmem = pltpu.VMEM

    sent, filters = call(
        forward_x_kernel,
        (device.reshape(1), outer(arrays[0]), outer(tables)),
        (pltpu.SMEM, pl.ANY, pl.ANY),
        [vmem((128, 2, 2, 8, 128), f32), vmem((2, 3, 136, 384), f32)],
        [
            vmem((2, 4, 64, 8, 128), f32),
            vmem((7, 256, 256), jnp.bfloat16),
            dma((2, 4)),
            dma,
        ],
        12,
    )
    received = exchange(sent.reshape(128, 32, 128), order)

    (sent,) = call(
        plane_kernel,
        (held(received.reshape(2, 2, 4, 4, 2, 2, 16, 128)), held(filters), held(tables)),
        (vmem, vmem, vmem),
        [vmem((2, 2, 4, 4, 2, 2, 2, 16, 128), f32)],
        [
            vmem((2, 8, 256, 128), f32),
            vmem((4, 256, 512), f32),
            vmem((2, 8, 2, 256, 128), f32),
        ],
        16,
    )
    received = exchange(sent.reshape(128, 64, 128), order)

    outs = call(
        update_kernel,
        (held(received.reshape(128, 2, 2, 2, 8, 128)), held(tables), *map(held, arrays)),
        (vmem,) * 9,
        [jax.ShapeDtypeStruct((64, 2, 8, 512), f32)] * 3,
        [
            vmem((2, 2, 4, 64, 8, 128), f32),
            vmem((2, 2, 64, 8, 512), f32),
            dma((2, 3, 4)),
        ],
        16,
    )
    return tuple(o.reshape(64, 16, 512) for o in outs)


def solution(mesh):
    spec = P("row", "col", None)
    return jax.shard_map(
        body, mesh=mesh, in_specs=(spec,) * 7, out_specs=(spec,) * 3, check_vma=False
    )
```
